256 devices in a mesh: prow: 32 (over y, x, core), pcol: 8 (over z).
Axes of the slice: x: 4, y: 4, z: 8, core: 2. Of those that a mesh axis runs over, the one named last changes fastest.
Arguments:
- eigvecs: float32 [65536, 4096], P('prow', 'pcol'), may hold values from -6 to 6
- reflectors: float32 [65536, 512], P('prow', 'pcol'), may hold values from -0.25 to 0.25
- factors: float32 [512, 256], P('pcol'), may hold values from -1 to 2, as said below
Outputs:
- result_vectors: float32 [65536, 4096], P('prow', 'pcol')
The draws below stay inside these ranges and needn't reach their ends.
Inputs may be any that keep to these rules, and one draw needn't show every extreme that they name: `factors`: within each block of 256 rows the factor is upper triangular, its diagonal between 1 and 2.
All inputs are finite; a program needn't handle non-finite values.
Results may differ from the reference program's by a relative error of at most 0.00017.
Values sent between devices are 32-bit elements; how exact they have to be, the bound alone decides.
A program may use at most 64 MiB of HBM per device.

```python
import jax
import jax.numpy as jnp
from jax import lax

K = 4096
NB = 256
NBLK = 2
N = 65536


def draw_factors(key, part):
    key = jax.random.fold_in(key, 7)
    first, second = jax.random.split(key)
    local_row = jnp.arange(NBLK * NB) % NB
    column = jnp.arange(NB)
    upper = column[None, :] > local_row[:, None]
    on_diag = column[None, :] == local_row[:, None]
    diag_values = jax.random.uniform(first, (NBLK * NB, NB), jnp.float32, 1.0, 2.0)
    off_values = jnp.clip(jax.random.normal(second, (NBLK * NB, NB), jnp.float32), -3.0, 3.0)
    off_values = off_values * (0.7 / NB ** 0.5)
    return jnp.where(on_diag, diag_values, jnp.where(upper, off_values, 0.0)).astype(jnp.float32)


def shard_levels(stream_key, shape, shards, smallest, high):
    gain = 1.0
    for axis_at, parts in shards:
        heights = jax.random.uniform(jax.random.fold_in(jax.random.fold_in(stream_key, 6), axis_at), (parts,), jnp.float32, smallest / len(shards), high / len(shards))
        gain = gain * jnp.repeat(jnp.exp(heights), shape[axis_at] // parts).reshape((-1,) + (1,) * (len(shape) - 1 - axis_at))
    return gain


def bell_draw(key, extent, deviation, bound, cuts=(), kind=jnp.bfloat16):
    level = shard_levels(key, extent, cuts, -0.22, 0.18) if cuts else 1.0
    values = jax.random.normal(key, extent, jnp.float32) * deviation * level
    return jnp.minimum(jnp.maximum(values, -bound), bound).astype(kind)


def setup_inputs(seed: int = 0) -> dict:
    keys = jax.random.split(jax.random.key(seed), 4)
    return {
        "eigvecs": bell_draw(keys[0], (N, K), 1.0, 6.0, ((0, 32), (1, 8)), jnp.float32),
        "reflectors": bell_draw(keys[1], (N, NBLK * NB), ((N * NB) ** -0.25), 0.25, ((0, 32), (1, 8)), jnp.float32),
        "factors": draw_factors(jax.random.fold_in(keys[3], 71), 0),
    }


def reference(eigvecs, reflectors, factors):
    highest = lax.Precision.HIGHEST
    vectors = eigvecs
    for index in range(NBLK - 1, -1, -1):
        panel = reflectors[:, index * NB:(index + 1) * NB]
        triangle = factors[index * NB:(index + 1) * NB]
        products = lax.dot_general(panel, vectors, (((0,), (0,)), ((), ())), precision=highest, preferred_element_type=jnp.float32)
        coeffs = jnp.dot(triangle, products, precision=highest, preferred_element_type=jnp.float32)
        vectors = vectors - jnp.dot(panel, coeffs, precision=highest, preferred_element_type=jnp.float32)
    return vectors
```

```python
import functools

import jax
import jax.numpy as jnp
from jax import lax
from jax.experimental import pallas as pl
from jax.experimental.pallas import tpu as pltpu
from jax.sharding import PartitionSpec as P

MESH = pl.DeviceIdType.MESH
F32, BF16 = jnp.float32, jnp.bfloat16
PLANES = 8
ROWS = 32
CHIPS = 16
SLAB = 64
PIECES = 2
NN = (((1,), (0,)), ((), ()))
NT = (((1,), (1,)), ((), ()))
TN = (((0,), (0,)), ((), ()))


def split(value):
    high = value.astype(BF16)
    return high, (value - high.astype(F32)).astype(BF16)


def product(left, right, dims):
    dot = functools.partial(lax.dot_general, dimension_numbers=dims, preferred_element_type=F32)
    return dot(left[0], right[0]) + (dot(left[1], right[0]) + dot(left[0], right[1]))


def kernel(
    z_hbm, v_hbm, t_hbm, out,
    panel, v_hi, v_lo, vt_hi, vt_lo, z_full, z_hi, z_lo, z_sum, gram,
    t_in, t_mine, t_planes, t_all, t_full, coeff, c_hi, c_lo,
    give_a, give_b, give_c, give_d, take_a, take_b, take_c, take_d, all_a, all_b, all_c, all_d,
    local, ring_out, ring_in, t_out, t_got, part_out, part_in,
):
    z, p = lax.axis_index("pcol"), lax.axis_index("prow")
    chip, core = p // 2, lax.rem(p, 2)
    right, left = lax.rem(z + 1, PLANES), lax.rem(z + PLANES - 1, PLANES)

    def plane(offset):
        return lax.rem(z + offset, PLANES)

    def mate(step):
        o = 20 + step
        o = o - 31 * (o // 32)
        y = lax.rem(p // 8 + o // 8, 4)
        x = lax.rem(chip + lax.rem(o // 2, 4), 4)
        return (y * 4 + x) * 2 + lax.rem(core + lax.rem(o, 2), 2)

    def fellow(step):
        o = 1 + step
        return (lax.rem(p // 8 + o // 4, 4) * 4 + lax.rem(chip + lax.rem(o, 4), 4)) * 2 + core

    barrier = pltpu.get_barrier_semaphore()
    for offset in range(1, PLANES):
        pl.semaphore_signal(barrier, inc=1, device_id={"pcol": plane(offset)}, device_id_type=MESH)

    def greet(step, carry):
        pl.semaphore_signal(barrier, inc=1, device_id={"prow": mate(step)}, device_id_type=MESH)
        return carry

    lax.fori_loop(0, ROWS - 1, greet, 0)
    own_copy = pltpu.make_async_copy(v_hbm, panel.at[z], local.at[0])
    t_copy = pltpu.make_async_copy(t_hbm, t_in, local.at[1])
    z_copy = pltpu.make_async_copy(z_hbm, z_full, local.at[2])
    own_copy.start()
    t_copy.start()
    z_copy.start()
    pl.semaphore_wait(barrier, PLANES - 1 + ROWS - 1)

    height = SLAB // PIECES

    def ring(way, step, piece):
        slab = plane(PLANES - step) if way == 0 else plane(step)
        ref = panel.at[slab, pl.ds(piece * height, height)]
        return pltpu.make_async_remote_copy(
            ref, ref, ring_out.at[way, step, piece], ring_in.at[way, step, piece],
            device_id={"pcol": right if way == 0 else left}, device_id_type=MESH,
        )

    def pieces(way, step):
        half = PIECES // 2
        if step < 3:
            return list(range(PIECES))
        return list(range(half)) if way == 0 else list(range(half, PIECES))

    def arrive(step):
        for piece in range(PIECES):
            for way in range(2):
                if piece in pieces(way, step):
                    ring(way, step, piece).wait_recv()
                if step < 3 and piece in pieces(way, step + 1):
                    ring(way, step + 1, piece).start()

    own_copy.wait()
    for piece in range(PIECES):
        for way in range(2):
            ring(way, 0, piece).start()

    t_copy.wait()
    for tile in range(CHIPS):
        t_mine[tile] = t_in[(tile // 2) * 8 : (tile // 2) * 8 + 8, (tile % 2) * 128 : (tile % 2) * 128 + 128]
    for offset in range(1, PLANES):
        pltpu.make_async_remote_copy(
            t_mine.at[chip], t_planes.at[z], t_out.at[0], t_got.at[0],
            device_id={"pcol": plane(offset)}, device_id_type=MESH,
        ).start()
    t_planes[z] = t_mine[chip]

    def t_wait(stage):
        ref = t_planes.at[pl.ds(0, PLANES - 1)] if stage == 0 else t_all.at[pl.ds(0, CHIPS - 1)]
        return pltpu.make_async_remote_copy(
            ref, ref, t_out.at[stage], t_got.at[stage], device_id={"pcol": right}, device_id_type=MESH
        )

    def t_spread():
        t_wait(0).wait_recv()

        def send(step, carry):
            pltpu.make_async_remote_copy(
                t_planes, t_all.at[chip], t_out.at[1], t_got.at[1],
                device_id={"prow": fellow(step)}, device_id_type=MESH,
            ).start()
            return carry

        lax.fori_loop(0, CHIPS - 1, send, 0)
        t_all[chip] = t_planes[...]

    def t_collect():
        t_wait(1).wait_recv()
        for tile in range(CHIPS):
            for slab in range(PLANES):
                t_full[
                    slab * SLAB + (tile // 2) * 8 : slab * SLAB + (tile // 2) * 8 + 8,
                    (tile % 2) * 128 : (tile % 2) * 128 + 128,
                ] = t_all[tile, slab]

    gives, takes, alls = (give_a, give_b, give_c, give_d), (take_a, take_b, take_c, take_d), (all_a, all_b, all_c, all_d)

    def part_wait(part, stage):
        ref = (takes, alls)[stage][part].at[pl.ds(0, ROWS - 1)]
        return pltpu.make_async_remote_copy(
            ref, ref, part_out.at[part, stage], part_in.at[part, stage],
            device_id={"pcol": right}, device_id_type=MESH,
        )

    def part_give(part):
        def send(step, carry):
            other = mate(step)
            pltpu.make_async_remote_copy(
                gives[part].at[other], takes[part].at[p], part_out.at[part, 0], part_in.at[part, 0],
                device_id={"prow": other}, device_id_type=MESH,
            ).start()
            return carry

        lax.fori_loop(0, ROWS - 1, send, 0)
        takes[part][p] = gives[part][p]

    def part_sum(part):
        part_wait(part, 0).wait_recv()
        alls[part][p] = jnp.sum(takes[part][...], axis=0)

        def send(step, carry):
            pltpu.make_async_remote_copy(
                alls[part].at[p], alls[part].at[p], part_out.at[part, 1], part_in.at[part, 1],
                device_id={"prow": mate(step)}, device_id_type=MESH,
            ).start()
            return carry

        lax.fori_loop(0, ROWS - 1, send, 0)

    def halves(slab):
        v_hi[slab], v_lo[slab] = split(panel[slab])

    def others(slab):
        at = pl.ds(4 - 4 * (slab // 4), 4)
        return v_hi[at].reshape(4 * SLAB, -1), v_lo[at].reshape(4 * SLAB, -1)

    def gram_of(slab):
        return product((v_hi[slab], v_lo[slab]), others(slab), NT)

    def sums_of(slabs):
        rows = len(slabs) * SLAB
        high = [v_hi[slab] for slab in slabs]
        low = [v_lo[slab] for slab in slabs]
        by_high = lax.dot_general(jnp.concatenate(high + low, axis=0), z_hi[...], NN, preferred_element_type=F32)
        by_low = lax.dot_general(jnp.concatenate(high, axis=0), z_lo[...], NN, preferred_element_type=F32)
        return by_high[:rows] + (by_high[rows:] + by_low)

    def lay_sums(part, values):
        for index in range(values.shape[0] // SLAB):
            for tile in range(ROWS):
                row, lane = index * SLAB + (tile // 4) * 8, (tile % 4) * 128
                gives[part][tile, index * 8 : index * 8 + 8] = values[row : row + 8, lane : lane + 128]

    def lay_gram(part, first, values, index):
        for tile in range(16):
            row, lane = (tile // 2) * 8, (tile % 2) * 128
            gives[part][index * 16 + tile, first : first + 8] = values[row : row + 8, lane : lane + 128]

    def collect(part, slabs):
        part_wait(part, 1).wait_recv()
        count = len(slabs)
        for index, slab in enumerate(slabs):
            for tile in range(ROWS):
                row, lane = (tile // 4) * 8, (tile % 4) * 128
                z_sum[slab, row : row + 8, lane : lane + 128] = alls[part][tile, index * 8 : index * 8 + 8]
        if part < 3:
            for index, slab in enumerate(slabs[-2:]):
                for tile in range(16):
                    row, lane = (tile // 2) * 8, (tile % 2) * 128
                    gram[slab, row : row + 8, lane : lane + 128] = alls[part][
                        index * 16 + tile, count * 8 : count * 8 + 8
                    ]
        else:
            for tile in range(32):
                row, lane = (tile // 4) * 8 + (tile % 2) * 4, (tile // 2 % 2) * 128
                gram[slabs[0], row : row + 4, lane : lane + 128] = alls[part][tile, 8:12]

    def turn(at, slabs):
        for target, source in ((vt_hi, v_hi), (vt_lo, v_lo)):
            target[:, at * 128 : at * 128 + 128] = jnp.concatenate([source[slab] for slab in slabs], axis=0).T

    late = plane(4)
    v_hi[...] = jnp.zeros_like(v_hi)
    v_lo[...] = jnp.zeros_like(v_lo)
    gram[z] = jnp.zeros_like(gram[z])
    halves(z)
    z_copy.wait()
    z_hi[...], z_lo[...] = split(z_full[...])

    for step in range(3):
        pair = [plane(PLANES - 1 - step), plane(1 + step)]
        slabs = [z, *pair] if step == 0 else pair
        arrive(step)
        halves(pair[0])
        first = gram_of(pair[0])
        halves(pair[1])
        second = gram_of(pair[1])
        lay_sums(step, sums_of(slabs))
        lay_gram(step, len(slabs) * 8, first, 0)
        lay_gram(step, len(slabs) * 8, second, 1)
        part_give(step)
        if step == 0:
            t_spread()
        if step == 1:
            t_collect()
        if step < 2:
            turn(step + 1, pair)
            part_sum(step)

    arrive(3)
    halves(late)
    grams = gram_of(late)
    lay_sums(3, sums_of([late]))
    for tile in range(32):
        row, lane = (tile // 4) * 8 + (tile % 2) * 4, (tile // 2 % 2) * 128
        give_d[tile, 8:12] = grams[row : row + 4, lane : lane + 128]
    part_give(3)
    part_sum(2)
    turn(0, [z, late])
    turn(3, [plane(5), plane(3)])
    collect(0, [z, plane(7), plane(1)])
    collect(1, [plane(6), plane(2)])
    part_sum(3)
    collect(2, [plane(5), plane(3)])
    t_hi, t_lo = split(t_full[...])
    collect(3, [late])

    sums = z_sum[...].reshape(512, -1)
    grams = split(gram[...].reshape(512, 256))
    second = product((t_hi[256:], t_lo[256:]), split(sums[256:]), NN)
    halved = split(second)
    crossed = product((grams[0][:256], grams[1][:256]), halved, NN) + product(
        (grams[0][256:], grams[1][256:]), halved, TN
    )
    first = product((t_hi[:256], t_lo[:256]), split(sums[:256] - crossed), NN)
    coeff[pl.ds(0, 4)] = first.reshape(4, SLAB, -1)
    coeff[pl.ds(4, 4)] = second.reshape(4, SLAB, -1)
    for index, offset in enumerate((0, 4, 7, 1, 6, 2, 5, 3)):
        high, low = split(coeff[plane(offset)])
        c_hi[index * SLAB : index * SLAB + SLAB] = high
        c_lo[index * SLAB : index * SLAB + SLAB] = low

    def finish(block, carry):
        at = pl.ds(pl.multiple_of(block * 256, 256), 256)
        update = product((vt_hi[at], vt_lo[at]), (c_hi[...], c_lo[...]), NN)
        out[at] = z_full[at] - update
        return carry

    lax.fori_loop(0, z_full.shape[0] // 256, finish, 0)

    for step in range(4):
        for way in range(2):
            for piece in pieces(way, step):
                ring(way, step, piece).wait_send()
    t_wait(0).wait_send()
    t_wait(1).wait_send()
    for part in range(4):
        part_wait(part, 0).wait_send()
        part_wait(part, 1).wait_send()


def shards(eigvecs, reflectors, factors):
    rows, columns = eigvecs.shape
    heights = (32, 24, 24, 12)
    scratch = [
        pltpu.VMEM((PLANES, SLAB, rows), F32),
        pltpu.VMEM((PLANES, SLAB, rows), BF16),
        pltpu.VMEM((PLANES, SLAB, rows), BF16),
        pltpu.VMEM((rows, PLANES * SLAB), BF16),
        pltpu.VMEM((rows, PLANES * SLAB), BF16),
        pltpu.VMEM((rows, columns), F32),
        pltpu.VMEM((rows, columns), BF16),
        pltpu.VMEM((rows, columns), BF16),
        pltpu.VMEM((PLANES, SLAB, columns), F32),
        pltpu.VMEM((PLANES, SLAB, 256), F32),
        pltpu.VMEM((SLAB, 256), F32),
        pltpu.VMEM((CHIPS, 8, 128), F32),
        pltpu.VMEM((PLANES, 8, 128), F32),
        pltpu.VMEM((CHIPS, PLANES, 8, 128), F32),
        pltpu.VMEM((PLANES * SLAB, 256), F32),
        pltpu.VMEM((PLANES, SLAB, columns), F32),
        pltpu.VMEM((PLANES * SLAB, columns), BF16),
        pltpu.VMEM((PLANES * SLAB, columns), BF16),
        *[pltpu.VMEM((ROWS, height, 128), F32) for _ in range(3) for height in heights],
        pltpu.SemaphoreType.DMA((3,)),
        pltpu.SemaphoreType.DMA((2, 4, PIECES)),
        pltpu.SemaphoreType.DMA((2, 4, PIECES)),
        pltpu.SemaphoreType.DMA((2,)),
        pltpu.SemaphoreType.DMA((2,)),
        pltpu.SemaphoreType.DMA((4, 2)),
        pltpu.SemaphoreType.DMA((4, 2)),
    ]
    return pl.pallas_call(
        kernel,
        out_shape=jax.ShapeDtypeStruct(eigvecs.shape, F32),
        in_specs=[pl.BlockSpec(memory_space=pl.ANY)] * 3,
        out_specs=pl.BlockSpec(memory_space=pltpu.VMEM),
        scratch_shapes=scratch,
        compiler_params=pltpu.CompilerParams(
            collective_id=0, has_side_effects=True, vmem_limit_bytes=48 * 1024 * 1024
        ),
    )(eigvecs, reflectors.T, factors)


def solution(mesh):
    return jax.shard_map(
        shards,
        mesh=mesh,
        in_specs=(P("prow", "pcol"), P("prow", "pcol"), P("pcol", None)),
        out_specs=P("prow", "pcol"),
        check_vma=False,
    )
```

```python
import functools

import jax
import jax.numpy as jnp
from jax import lax
from jax.experimental import pallas as pl
from jax.experimental.pallas import tpu as pltpu
from jax.sharding import PartitionSpec as P

MESH = pl.DeviceIdType.MESH
F32, BF16 = jnp.float32, jnp.bfloat16
PLANES = 8
ROWS = 32
CHIPS = 16
SLAB = 64
HALF = SLAB // 2
NN = (((1,), (0,)), ((), ()))
NT = (((1,), (1,)), ((), ()))
TN = (((0,), (0,)), ((), ()))
PARTS = ((6, 4), (4, 4), (2, 2), (2, 2), (2, 2))
LAST = len(PARTS) - 1
HEIGHTS = tuple(4 * pieces + 2 * grams for pieces, grams in PARTS)


def split(value):
    high = value.astype(BF16)
    return high, (value - high.astype(F32)).astype(BF16)


def product(left, right, dims):
    dot = functools.partial(lax.dot_general, dimension_numbers=dims, preferred_element_type=F32)
    return dot(left[0], right[0]) + (dot(left[1], right[0]) + dot(left[0], right[1]))


def stacked(left, right, dims):
    rows = left[0].shape[0]
    by_high = lax.dot_general(jnp.concatenate(left, axis=0), right[0], dims, preferred_element_type=F32)
    by_low = lax.dot_general(left[0], right[1], dims, preferred_element_type=F32)
    return by_high[:rows] + (by_high[rows:] + by_low)


def kernel(
    z_hbm, v_hbm, t_hbm, z_full, v_hi, v_lo, c_hi, c_lo,
    panel, z_hi, z_lo, z_sum, gram, t_in, t_mine, t_planes, t_all, t_full,
    local, ring_out, ring_in, t_sem, t_spread_sem, part_out, part_in, *buffers,
):
    z, p = lax.axis_index("pcol"), lax.axis_index("prow")
    chip, core = p // 2, lax.rem(p, 2)
    right, left = lax.rem(z + 1, PLANES), lax.rem(z + PLANES - 1, PLANES)
    twin = p + 1 - 2 * core
    count = len(PARTS)
    gives, mixes, takes, alls = (buffers[i * count : i * count + count] for i in range(4))

    def plane(offset):
        return lax.rem(z + offset, PLANES)

    def fellow(step):
        o = 10 + step
        o = o - 15 * (o // 16)
        return (lax.rem(p // 8 + o // 4, 4) * 4 + lax.rem(chip + lax.rem(o, 4), 4)) * 2 + core

    barrier = pltpu.get_barrier_semaphore()
    for offset in (1, 7, 2, 6, 3, 5, 4):
        pl.semaphore_signal(barrier, inc=1, device_id={"pcol": plane(offset)}, device_id_type=MESH)
    pl.semaphore_signal(barrier, inc=1, device_id={"prow": twin}, device_id_type=MESH)

    def greet(step, carry):
        pl.semaphore_signal(barrier, inc=1, device_id={"prow": fellow(step)}, device_id_type=MESH)
        return carry

    lax.fori_loop(0, CHIPS - 1, greet, 0)
    t_copy = pltpu.make_async_copy(t_hbm, t_in, local.at[0])
    own_copy = pltpu.make_async_copy(v_hbm, panel.at[z], local.at[1])
    z_copy = pltpu.make_async_copy(z_hbm, z_full, local.at[2])
    t_copy.start()
    own_copy.start()
    z_copy.start()
    pl.semaphore_wait(barrier, CHIPS + PLANES - 1)

    def ring(way, step, half):
        rows = pl.ds(half * HALF, HALF)
        ref = panel.at[plane(PLANES - step) if way == 0 else plane(step), rows]
        return pltpu.make_async_remote_copy(
            v_hbm.at[rows] if step == 0 else ref, ref, ring_out.at[way, step, half], ring_in.at[way, step, half],
            device_id={"pcol": right if way == 0 else left}, device_id_type=MESH,
        )

    def arrive(step, half):
        for way in range(2):
            ring(way, step, half).wait_recv()
            if step < 2 or half == way:
                ring(way, step + 1, half).start()

    for half in range(2):
        for way in range(2):
            ring(way, 0, half).start()

    t_copy.wait()
    for tile in range(CHIPS):
        t_mine[tile] = t_in[(tile // 2) * 8 : (tile // 2) * 8 + 8, (tile % 2) * 128 : (tile % 2) * 128 + 128]
    for offset in range(1, PLANES):
        pltpu.make_async_remote_copy(
            t_mine.at[chip], t_planes.at[z], t_sem.at[0], t_sem.at[1],
            device_id={"pcol": plane(offset)}, device_id_type=MESH,
        ).start()
    t_planes[z] = t_mine[chip]

    def t_wait_planes():
        ref = t_planes.at[pl.ds(0, PLANES - 1)]
        return pltpu.make_async_remote_copy(
            ref, ref, t_sem.at[0], t_sem.at[1], device_id={"pcol": right}, device_id_type=MESH
        )

    def t_wait():
        ref = t_all.at[pl.ds(0, CHIPS - 1)]
        return pltpu.make_async_remote_copy(
            ref, ref, t_spread_sem.at[0], t_spread_sem.at[1], device_id={"pcol": right}, device_id_type=MESH
        )

    def t_spread():
        t_wait_planes().wait_recv()

        def send(step, carry):
            pltpu.make_async_remote_copy(
                t_planes, t_all.at[chip], t_spread_sem.at[0], t_spread_sem.at[1],
                device_id={"prow": fellow(step)}, device_id_type=MESH,
            ).start()
            return carry

        lax.fori_loop(0, CHIPS - 1, send, 0)
        t_all[chip] = t_planes[...]

    def t_collect():
        t_wait().wait_recv()
        for tile in range(CHIPS):
            for slab in range(PLANES):
                t_full[
                    slab * SLAB + (tile // 2) * 8 : slab * SLAB + (tile // 2) * 8 + 8,
                    (tile % 2) * 128 : (tile % 2) * 128 + 128,
                ] = t_all[tile, slab]

    def to_twin(part, stage, source, target):
        return pltpu.make_async_remote_copy(
            source, target, part_out.at[part, stage], part_in.at[part, stage],
            device_id={"prow": twin}, device_id_type=MESH,
        )

    def to_fellows(part, stage, source, target):
        def send(step, carry):
            other = fellow(step)
            pltpu.make_async_remote_copy(
                source(other // 2), target, part_out.at[part, stage], part_in.at[part, stage],
                device_id={"prow": other}, device_id_type=MESH,
            ).start()
            return carry

        lax.fori_loop(0, CHIPS - 1, send, 0)

    def from_fellows(part, stage):
        ref = takes[part].at[pl.ds(0, CHIPS - 1)]
        return pltpu.make_async_remote_copy(
            ref, ref, part_out.at[part, stage], part_in.at[part, stage],
            device_id={"prow": twin}, device_id_type=MESH,
        )

    def mix_copy(part):
        if part < LAST:
            return to_twin(part, 0, gives[part].at[1 - core], mixes[part].at[0])
        return to_twin(part, 0, mixes[part].at[0], mixes[part].at[1])

    def back_copy(part):
        return to_twin(part, 3, alls[part].at[core], alls[part].at[core])

    def scatter(part):
        give, take = gives[part], takes[part]
        if part < LAST:
            mix_copy(part).wait_recv()
            mixes[part][1] = give[core] + mixes[part][0]
            give = mixes[part].at[1]
        to_fellows(part, 1, lambda other: give.at[other], take.at[chip])
        take[chip] = give[chip]

    def gather(part):
        from_fellows(part, 1).wait_recv()
        total = jnp.sum(takes[part][...], axis=0)
        if part < LAST:
            kept = alls[part].at[core]
        else:
            kept, mix = alls[part], mixes[part]
            mix[0] = total
            copy = mix_copy(part)
            copy.start()
            copy.wait_recv()
            total = total + mix[1]
        kept[chip] = total
        to_fellows(part, 2, lambda other: kept.at[chip], kept.at[chip])

    def give_back(part):
        from_fellows(part, 2).wait_recv()
        back_copy(part).start()

    def place(part, tile):
        return (tile % 2, tile // 2) if part < LAST else (tile // 2, tile % 2)

    def halves(slab, first=0, rows=SLAB):
        at = pl.ds(first, rows)
        v_hi[slab, at], v_lo[slab, at] = split(panel[slab, at])

    def gram_of(slab, first=0, rows=SLAB):
        at, others = pl.ds(first, rows), pl.ds(4 - 4 * (slab // 4), 4)
        whole = (v_hi[others].reshape(4 * SLAB, -1), v_lo[others].reshape(4 * SLAB, -1))
        return stacked((v_hi[slab, at], v_lo[slab, at]), whole, NT)

    def sums_of(pieces):
        high, low = ([ref[slab, pl.ds(first, rows)] for slab, first, rows in pieces] for ref in (v_hi, v_lo))
        together = functools.partial(jnp.concatenate, axis=0)
        return stacked((together(high), together(low)), (z_hi[...], z_lo[...]), NN)

    def lay(part, sums, grams):
        pieces, with_gram = PARTS[part]
        for index in range(pieces * 16):
            tile, slot = place(part, index % ROWS), index // ROWS * 8
            row, lane = index // 4 * 8, index % 4 * 128
            gives[part].at[*tile][slot : slot + 8] = sums[row : row + 8, lane : lane + 128]
        for index in range(with_gram * 16):
            tile, slot = place(part, index % ROWS), pieces * 4 + index // ROWS * 4
            row, lane = index // 2 * 4, index % 2 * 128
            gives[part].at[*tile][slot : slot + 4] = grams[row : row + 4, lane : lane + 128]

    def collect(part, slabs):
        if part < LAST:
            back_copy(part).wait_recv()
        else:
            from_fellows(part, 2).wait_recv()
        pieces, with_gram = PARTS[part]
        for index in range(pieces * 16):
            tile, slot = place(part, index % ROWS), index // ROWS * 8
            slab, first = slabs[index // 16]
            row, lane = first + index % 16 // 4 * 8, index % 4 * 128
            z_sum[slab, row : row + 8, lane : lane + 128] = alls[part][*tile, slot : slot + 8]
        for index in range(with_gram * 16):
            tile, slot = place(part, index % ROWS), pieces * 4 + index // ROWS * 4
            slab, first = slabs[pieces - with_gram + index // 16]
            row, lane = first + index % 16 // 2 * 4, index % 2 * 128
            gram[slab, row : row + 4, lane : lane + 128] = alls[part][*tile, slot : slot + 4]

    def both(slab):
        return [(slab, 0), (slab, HALF)]

    def compute(part, fresh, older=()):
        grams = []
        for piece in fresh:
            halves(*piece)
            grams.append(gram_of(*piece))
        lay(part, sums_of([*older, *fresh]), jnp.concatenate(grams, axis=0))
        if part < LAST:
            mix_copy(part).start()

    behind = [plane(PLANES - 1 - step) for step in range(3)]
    ahead = [plane(1 + step) for step in range(3)]
    late = plane(4)
    v_hi[...] = jnp.zeros_like(v_hi)
    v_lo[...] = jnp.zeros_like(v_lo)
    gram[z] = jnp.zeros_like(gram[z])
    own_copy.wait()
    halves(z)
    z_copy.wait()
    z_hi[...], z_lo[...] = split(z_full[...])

    arrive(0, 0)
    arrive(0, 1)
    compute(0, [(behind[0], 0, SLAB), (ahead[0], 0, SLAB)], [(z, 0, SLAB)])
    scatter(0)
    arrive(1, 0)
    gather(0)
    t_spread()
    arrive(1, 1)
    compute(1, [(behind[1], 0, SLAB), (ahead[1], 0, SLAB)])
    scatter(1)
    arrive(2, 0)
    compute(2, [(behind[2], 0, HALF), (ahead[2], 0, HALF)])
    give_back(0)
    gather(1)
    scatter(2)
    t_collect()
    arrive(2, 1)
    compute(3, [(behind[2], HALF, HALF), (ahead[2], HALF, HALF)])
    scatter(3)
    gather(2)
    ring(0, 3, 0).wait_recv()
    ring(1, 3, 1).wait_recv()
    compute(4, [(late, 0, SLAB)])
    scatter(4)
    give_back(1)
    gather(3)
    collect(0, both(z) + both(behind[0]) + both(ahead[0]))
    t_hi, t_lo = split(t_full[...])
    give_back(2)
    collect(1, both(behind[1]) + both(ahead[1]))
    gather(4)
    give_back(3)
    collect(2, [(behind[2], 0), (ahead[2], 0)])
    collect(3, [(behind[2], HALF), (ahead[2], HALF)])
    collect(4, both(late))

    sums = z_sum[...].reshape(2 * 4 * SLAB, -1)
    grams = split(gram[...].reshape(2 * 4 * SLAB, -1))
    upper, lower = slice(0, 4 * SLAB), slice(4 * SLAB, 8 * SLAB)
    second = product((t_hi[lower], t_lo[lower]), split(sums[lower]), NN)
    parted = split(second)
    crossed = product((grams[0][upper], grams[1][upper]), parted, NN) + product(
        (grams[0][lower], grams[1][lower]), parted, TN
    )
    first = product((t_hi[upper], t_lo[upper]), split(sums[upper] - crossed), NN)
    c_hi[lower], c_lo[lower] = parted
    c_hi[upper], c_lo[upper] = split(first)

    for step in range(4):
        for way in range(2):
            for half in range(2):
                if step < 3 or half == way:
                    ring(way, step, half).wait_send()
    t_wait_planes().wait_send()
    t_wait().wait_send()
    for part in range(count):
        mix_copy(part).wait_send()
        from_fellows(part, 1).wait_send()
        from_fellows(part, 2).wait_send()
        if part < LAST:
            back_copy(part).wait_send()


def finish(z_full, v_hi, v_lo, c_hi, c_lo, out, stage, sem):
    block = stage.shape[1]
    c = (c_hi[...], c_lo[...])
    copies = []
    for index in range(stage.shape[0]):
        at = pl.ds(index * block, block)
        v = tuple(ref[:, :, at].reshape(PLANES * SLAB, block) for ref in (v_hi, v_lo))
        stage[index] = z_full[at] - product(v, c, TN)
        copies.append(pltpu.make_async_copy(stage.at[index], out.at[at], sem.at[index]))
        copies[-1].start()
    for copy in copies:
        copy.wait()


def shards(eigvecs, reflectors, factors):
    rows, columns = eigvecs.shape
    width = PLANES * SLAB // 2
    scratch = [
        pltpu.VMEM((PLANES, SLAB, rows), F32),
        pltpu.VMEM((rows, columns), BF16),
        pltpu.VMEM((rows, columns), BF16),
        pltpu.VMEM((PLANES, SLAB, columns), F32),
        pltpu.VMEM((PLANES, SLAB, width), F32),
        pltpu.VMEM((SLAB, width), F32),
        pltpu.VMEM((CHIPS, 8, 128), F32),
        pltpu.VMEM((PLANES, 8, 128), F32),
        pltpu.VMEM((CHIPS, PLANES, 8, 128), F32),
        pltpu.VMEM((PLANES * SLAB, width), F32),
        pltpu.SemaphoreType.DMA((3,)),
        pltpu.SemaphoreType.DMA((2, 4, 2)),
        pltpu.SemaphoreType.DMA((2, 4, 2)),
        pltpu.SemaphoreType.DMA((2,)),
        pltpu.SemaphoreType.DMA((2,)),
        pltpu.SemaphoreType.DMA((len(PARTS), 4)),
        pltpu.SemaphoreType.DMA((len(PARTS), 4)),
    ]
    early, last = HEIGHTS[:-1], HEIGHTS[-1]
    scratch += [pltpu.VMEM((2, CHIPS, height, 128), F32) for height in early]
    scratch += [pltpu.VMEM((CHIPS, 2, last, 128), F32)]
    scratch += [pltpu.VMEM((2, CHIPS, height, 128), F32) for height in early]
    scratch += [pltpu.VMEM((2, 2, last, 128), F32)]
    scratch += [pltpu.VMEM((CHIPS, height, 128), F32) for height in early]
    scratch += [pltpu.VMEM((CHIPS, 2, last, 128), F32)]
    scratch += [pltpu.VMEM((2, CHIPS, height, 128), F32) for height in early]
    scratch += [pltpu.VMEM((CHIPS, 2, last, 128), F32)]
    held = pl.pallas_call(
        kernel,
        out_shape=[
            jax.ShapeDtypeStruct((rows, columns), F32),
            jax.ShapeDtypeStruct((PLANES, SLAB, rows), BF16),
            jax.ShapeDtypeStruct((PLANES, SLAB, rows), BF16),
            jax.ShapeDtypeStruct((PLANES * SLAB, columns), BF16),
            jax.ShapeDtypeStruct((PLANES * SLAB, columns), BF16),
        ],
        in_specs=[pl.BlockSpec(memory_space=pltpu.HBM)] * 3,
        out_specs=[pl.BlockSpec(memory_space=pltpu.VMEM)] * 5,
        scratch_shapes=scratch,
        compiler_params=pltpu.CompilerParams(
            collective_id=0, has_side_effects=True, vmem_limit_bytes=40 * 1024 * 1024
        ),
    )(*(pltpu.with_memory_space_constraint(array, pltpu.HBM) for array in (eigvecs, reflectors.T, factors)))
    blocks = 8
    return pl.pallas_call(
        finish,
        out_shape=jax.ShapeDtypeStruct((rows, columns), F32),
        in_specs=[pl.BlockSpec(memory_space=pltpu.VMEM)] * 5,
        out_specs=pl.BlockSpec(memory_space=pltpu.HBM),
        scratch_shapes=[
            pltpu.VMEM((blocks, rows // blocks, columns), F32),
            pltpu.SemaphoreType.DMA((blocks,)),
        ],
        compiler_params=pltpu.CompilerParams(vmem_limit_bytes=32 * 1024 * 1024),
    )(*held)


def solution(mesh):
    return jax.shard_map(
        shards,
        mesh=mesh,
        in_specs=(P("prow", "pcol"), P("prow", "pcol"), P("pcol", None)),
        out_specs=P("prow", "pcol"),
        check_vma=False,
    )
```

```python
import functools

import jax
import jax.numpy as jnp
from jax import lax
from jax.experimental import pallas as pl
from jax.experimental.pallas import tpu as pltpu
from jax.sharding import PartitionSpec as P

MESH = pl.DeviceIdType.MESH
F32, BF16 = jnp.float32, jnp.bfloat16
PLANES = 8
ROWS = 32
CHIPS = 16
SLAB = 64
HALF = SLAB // 2
NN = (((1,), (0,)), ((), ()))
NT = (((1,), (1,)), ((), ()))
TN = (((0,), (0,)), ((), ()))
PARTS = ((6, 4), (4, 4), (2, 2), (2, 2), (2, 2))
LAST = len(PARTS) - 1
HEIGHTS = tuple(4 * pieces + 2 * grams for pieces, grams in PARTS)


def split(value):
    high = value.astype(BF16)
    return high, (value - high.astype(F32)).astype(BF16)


def product(left, right, dims):
    dot = functools.partial(lax.dot_general, dimension_numbers=dims, preferred_element_type=F32)
    return dot(left[0], right[0]) + (dot(left[1], right[0]) + dot(left[0], right[1]))


def stacked(left, right, dims):
    rows = left[0].shape[0]
    by_high = lax.dot_general(jnp.concatenate(left, axis=0), right[0], dims, preferred_element_type=F32)
    by_low = lax.dot_general(left[0], right[1], dims, preferred_element_type=F32)
    return by_high[:rows] + (by_high[rows:] + by_low)


def kernel(
    z_hbm, v_hbm, t_hbm, z_full, v_hi, v_lo, c_hi, c_lo,
    panel, z_hi, z_lo, z_sum, gram, t_in, t_mine, t_planes, t_all, t_full,
    local, ring_out, ring_in, t_out, t_got, t_spread_sem, part_out, part_in, *buffers,
):
    z, p = lax.axis_index("pcol"), lax.axis_index("prow")
    chip, core = p // 2, lax.rem(p, 2)
    right, left = lax.rem(z + 1, PLANES), lax.rem(z + PLANES - 1, PLANES)
    twin = p + 1 - 2 * core
    count = len(PARTS)
    gives, takes, alls = (buffers[i * count : i * count + count] for i in range(3))
    mixes = buffers[3 * count :]

    def plane(offset):
        return lax.rem(z + offset, PLANES)

    ys, xs = ([lax.rem(at + offset, 4) for offset in range(4)] for at in (p // 8, chip))
    offsets = [(y, x) for y in (2, 1, 3, 0) for x in (2, 1, 3, 0)]
    offsets.sort(key=lambda at: -sum(min(step, 4 - step) for step in at))
    fellows = [(ys[y] * 4 + xs[x]) * 2 + core for y, x in offsets[:-1]]
    mates = [(ys[y] * 4 + xs[x]) * 2 + at for y, x in offsets for at in (1 - core, core)][:-1]

    barrier = pltpu.get_barrier_semaphore()
    for neighbour in (left, right):
        pl.semaphore_signal(barrier, inc=1, device_id={"pcol": neighbour}, device_id_type=MESH)

    for other in mates:
        pl.semaphore_signal(barrier, inc=1, device_id={"prow": other}, device_id_type=MESH)
    t_copy = pltpu.make_async_copy(t_hbm, t_in, local.at[0])
    own_copy = pltpu.make_async_copy(v_hbm, panel.at[z], local.at[1])
    z_copy = pltpu.make_async_copy(z_hbm, z_full, local.at[2])
    t_copy.start()
    own_copy.start()
    z_copy.start()
    pl.semaphore_wait(barrier, 2 + ROWS - 1)

    def ring(way, step, half):
        rows = pl.ds(half * HALF, HALF)
        ref = panel.at[plane(PLANES - step) if way == 0 else plane(step), rows]
        return pltpu.make_async_remote_copy(
            v_hbm.at[rows] if step == 0 else ref, ref, ring_out.at[way, step, half], ring_in.at[way, step, half],
            device_id={"pcol": right if way == 0 else left}, device_id_type=MESH,
        )

    def arrive(step, turn):
        for way in range(2):
            half = turn if way == 0 else 1 - turn
            ring(way, step, half).wait_recv()
            if step < 2 or (step == 2 and half == way):
                ring(way, step + 1, half).start()

    for turn in range(2):
        for way in range(2):
            ring(way, 0, turn if way == 0 else 1 - turn).start()

    def t_ring(way, step):
        ref = t_planes.at[plane(PLANES - step) if way == 0 else plane(step)]
        return pltpu.make_async_remote_copy(
            ref, ref, t_out.at[way, step], t_got.at[way, step],
            device_id={"pcol": right if way == 0 else left}, device_id_type=MESH,
        )

    def t_arrive(step):
        for way in range(2):
            if step + way < 4:
                t_ring(way, step).wait_recv()
            if step + way < 3:
                t_ring(way, step + 1).start()

    t_copy.wait()
    for index in range(ROWS):
        row, lane = index // 4 * 8 + index % 2 * 4, index // 2 % 2 * 128
        t_mine[index] = t_in[row : row + 4, lane : lane + 128]
    t_planes[z] = t_mine[p]
    for way in range(2):
        t_ring(way, 0).start()
    def t_wait():
        ref = t_all.at[pl.ds(0, ROWS - 1)]
        return pltpu.make_async_remote_copy(
            ref, ref, t_spread_sem.at[0], t_spread_sem.at[1], device_id={"pcol": right}, device_id_type=MESH
        )

    def t_spread():
        for other in mates:
            pltpu.make_async_remote_copy(
                t_planes, t_all.at[p], t_spread_sem.at[0], t_spread_sem.at[1],
                device_id={"prow": other}, device_id_type=MESH,
            ).start()
        t_all[p] = t_planes[...]

    def t_collect():
        t_wait().wait_recv()
        for index in range(ROWS):
            for slab in range(PLANES):
                row, lane = slab * SLAB + index // 4 * 8 + index % 2 * 4, index // 2 % 2 * 128
                t_full[row : row + 4, lane : lane + 128] = t_all[index, slab]

    def to_twin(part, stage, source, target):
        return pltpu.make_async_remote_copy(
            source, target, part_out.at[part, stage], part_in.at[part, stage],
            device_id={"prow": twin}, device_id_type=MESH,
        )

    def to_others(part, stage, source, target):
        for other in fellows if part < LAST else mates:
            pltpu.make_async_remote_copy(
                source(other // 2 if part < LAST else other), target, part_out.at[part, stage], part_in.at[part, stage],
                device_id={"prow": other}, device_id_type=MESH,
            ).start()

    def from_others(part, stage):
        ref = takes[part].at[pl.ds(0, takes[part].shape[0] - 1)]
        return pltpu.make_async_remote_copy(
            ref, ref, part_out.at[part, stage], part_in.at[part, stage],
            device_id={"prow": twin}, device_id_type=MESH,
        )

    def mix_copy(part):
        return to_twin(part, 0, gives[part].at[1 - core], mixes[part].at[0])

    def back_copy(part):
        return to_twin(part, 3, alls[part].at[core], alls[part].at[core])

    def scatter(part):
        give, take, me = gives[part], takes[part], chip if part < LAST else p
        if part < LAST:
            mix_copy(part).wait_recv()
            mixes[part][1] = give[core] + mixes[part][0]
            give = mixes[part].at[1]
        to_others(part, 1, lambda other: give.at[other], take.at[me])
        take[me] = give[me]

    def gather(part):
        from_others(part, 1).wait_recv()
        kept, me = (alls[part].at[core], chip) if part < LAST else (alls[part], p)
        kept[me] = jnp.sum(takes[part][...], axis=0)
        to_others(part, 2, lambda other: kept.at[me], kept.at[me])

    def give_back(part):
        from_others(part, 2).wait_recv()
        back_copy(part).start()

    def place(part, tile):
        return (tile % 2, tile // 2) if part < LAST else (tile,)

    def halves(slab, first=0, rows=SLAB):
        at = pl.ds(first, rows)
        v_hi[slab, at], v_lo[slab, at] = split(panel[slab, at])

    def gram_of(slab, first=0, rows=SLAB):
        at, others = pl.ds(first, rows), pl.ds(4 - 4 * (slab // 4), 4)
        whole = (v_hi[others].reshape(4 * SLAB, -1), v_lo[others].reshape(4 * SLAB, -1))
        return stacked((v_hi[slab, at], v_lo[slab, at]), whole, NT)

    def sums_of(pieces):
        high, low = ([ref[slab, pl.ds(first, rows)] for slab, first, rows in pieces] for ref in (v_hi, v_lo))
        together = functools.partial(jnp.concatenate, axis=0)
        return stacked((together(high), together(low)), (z_hi[...], z_lo[...]), NN)

    def lay(part, sums, grams):
        pieces, with_gram = PARTS[part]
        for index in range(pieces * 16):
            tile, slot = place(part, index % ROWS), index // ROWS * 8
            row, lane = index // 4 * 8, index % 4 * 128
            gives[part].at[*tile][slot : slot + 8] = sums[row : row + 8, lane : lane + 128]
        for index in range(with_gram * 16):
            tile, slot = place(part, index % ROWS), pieces * 4 + index // ROWS * 4
            row, lane = index // 2 * 4, index % 2 * 128
            gives[part].at[*tile][slot : slot + 4] = grams[row : row + 4, lane : lane + 128]

    def collect(part, slabs):
        if part < LAST:
            back_copy(part).wait_recv()
        else:
            from_others(part, 2).wait_recv()
        pieces, with_gram = PARTS[part]
        for index in range(pieces * 16):
            tile, slot = place(part, index % ROWS), index // ROWS * 8
            slab, first = slabs[index // 16]
            row, lane = first + index % 16 // 4 * 8, index % 4 * 128
            z_sum[slab, row : row + 8, lane : lane + 128] = alls[part][*tile, slot : slot + 8]
        for index in range(with_gram * 16):
            tile, slot = place(part, index % ROWS), pieces * 4 + index // ROWS * 4
            slab, first = slabs[pieces - with_gram + index // 16]
            row, lane = first + index % 16 // 2 * 4, index % 2 * 128
            gram[slab, row : row + 4, lane : lane + 128] = alls[part][*tile, slot : slot + 4]

    def both(slab):
        return [(slab, 0), (slab, HALF)]

    def compute(part, fresh, older=()):
        grams = []
        for piece in fresh:
            halves(*piece)
            grams.append(gram_of(*piece))
        lay(part, sums_of([*older, *fresh]), jnp.concatenate(grams, axis=0))
        if part < LAST:
            mix_copy(part).start()

    behind = [plane(PLANES - 1 - step) for step in range(3)]
    ahead = [plane(1 + step) for step in range(3)]
    late = plane(4)
    v_hi[...] = jnp.zeros_like(v_hi)
    v_lo[...] = jnp.zeros_like(v_lo)
    gram[z] = jnp.zeros_like(gram[z])
    own_copy.wait()
    halves(z)
    z_copy.wait()
    z_hi[...], z_lo[...] = split(z_full[...])

    arrive(0, 0)
    t_arrive(0)
    arrive(0, 1)
    compute(0, [(behind[0], 0, SLAB), (ahead[0], 0, SLAB)], [(z, 0, SLAB)])
    t_arrive(1)
    arrive(1, 0)
    scatter(0)
    t_arrive(2)
    arrive(1, 1)
    compute(1, [(behind[1], 0, SLAB), (ahead[1], 0, SLAB)])
    gather(0)
    t_arrive(3)
    arrive(2, 0)
    t_spread()
    scatter(1)
    compute(2, [(behind[2], 0, HALF), (ahead[2], HALF, HALF)])
    scatter(2)
    arrive(2, 1)
    compute(3, [(behind[2], HALF, HALF), (ahead[2], 0, HALF)])
    give_back(0)
    gather(1)
    scatter(3)
    gather(2)
    arrive(3, 0)
    compute(4, [(late, 0, SLAB)])
    scatter(4)
    collect(0, both(z) + both(behind[0]) + both(ahead[0]))
    gather(3)
    t_collect()
    t_hi, t_lo = split(t_full[...])
    give_back(1)
    give_back(2)
    collect(1, both(behind[1]) + both(ahead[1]))
    gather(4)
    give_back(3)
    collect(2, [(behind[2], 0), (ahead[2], HALF)])
    collect(3, [(behind[2], HALF), (ahead[2], 0)])
    collect(4, both(late))

    sums = z_sum[...].reshape(2 * 4 * SLAB, -1)
    grams = split(gram[...].reshape(2 * 4 * SLAB, -1))
    upper, lower = slice(0, 4 * SLAB), slice(4 * SLAB, 8 * SLAB)
    second = product((t_hi[lower], t_lo[lower]), split(sums[lower]), NN)
    parted = split(second)
    crossed = product((grams[0][upper], grams[1][upper]), parted, NN) + product(
        (grams[0][lower], grams[1][lower]), parted, TN
    )
    first = product((t_hi[upper], t_lo[upper]), split(sums[upper] - crossed), NN)
    c_hi[lower], c_lo[lower] = parted
    c_hi[upper], c_lo[upper] = split(first)

    for step in range(4):
        for way in range(2):
            for half in range(2):
                if step < 3 or half == way:
                    ring(way, step, half).wait_send()
    for step in range(4):
        for way in range(2):
            if step + way < 4:
                t_ring(way, step).wait_send()
    t_wait().wait_send()
    for part in range(count):
        from_others(part, 1).wait_send()
        from_others(part, 2).wait_send()
        if part < LAST:
            mix_copy(part).wait_send()
            back_copy(part).wait_send()


def finish(z_full, v_hi, v_lo, c_hi, c_lo, out, stage, sem):
    block = stage.shape[1]
    c = (c_hi[...], c_lo[...])
    copies = []
    for index in range(stage.shape[0]):
        at = pl.ds(index * block, block)
        v = tuple(ref[:, :, at].reshape(PLANES * SLAB, block) for ref in (v_hi, v_lo))
        stage[index] = z_full[at] - product(v, c, TN)
        copies.append(pltpu.make_async_copy(stage.at[index], out.at[at], sem.at[index]))
        copies[-1].start()
    for copy in copies:
        copy.wait()


def shards(eigvecs, reflectors, factors):
    rows, columns = eigvecs.shape
    width = PLANES * SLAB // 2
    scratch = [
        pltpu.VMEM((PLANES, SLAB, rows), F32),
        pltpu.VMEM((rows, columns), BF16),
        pltpu.VMEM((rows, columns), BF16),
        pltpu.VMEM((PLANES, SLAB, columns), F32),
        pltpu.VMEM((PLANES, SLAB, width), F32),
        pltpu.VMEM((SLAB, width), F32),
        pltpu.VMEM((ROWS, 4, 128), F32),
        pltpu.VMEM((PLANES, 4, 128), F32),
        pltpu.VMEM((ROWS, PLANES, 4, 128), F32),
        pltpu.VMEM((PLANES * SLAB, width), F32),
        pltpu.SemaphoreType.DMA((3,)),
        pltpu.SemaphoreType.DMA((2, 4, 2)),
        pltpu.SemaphoreType.DMA((2, 4, 2)),
        pltpu.SemaphoreType.DMA((2, 4)),
        pltpu.SemaphoreType.DMA((2, 4)),
        pltpu.SemaphoreType.DMA((2,)),
        pltpu.SemaphoreType.DMA((len(PARTS), 4)),
        pltpu.SemaphoreType.DMA((len(PARTS), 4)),
    ]
    early, last = HEIGHTS[:-1], pltpu.VMEM((ROWS, HEIGHTS[-1], 128), F32)
    paired = [pltpu.VMEM((2, CHIPS, height, 128), F32) for height in early]
    single = [pltpu.VMEM((CHIPS, height, 128), F32) for height in early]
    scratch += [*paired, last, *single, last, *paired, last, *paired]
    held = pl.pallas_call(
        kernel,
        out_shape=[
            jax.ShapeDtypeStruct((rows, columns), F32),
            jax.ShapeDtypeStruct((PLANES, SLAB, rows), BF16),
            jax.ShapeDtypeStruct((PLANES, SLAB, rows), BF16),
            jax.ShapeDtypeStruct((PLANES * SLAB, columns), BF16),
            jax.ShapeDtypeStruct((PLANES * SLAB, columns), BF16),
        ],
        in_specs=[pl.BlockSpec(memory_space=pltpu.HBM)] * 3,
        out_specs=[pl.BlockSpec(memory_space=pltpu.VMEM)] * 5,
        scratch_shapes=scratch,
        compiler_params=pltpu.CompilerParams(
            collective_id=0, has_side_effects=True, vmem_limit_bytes=40 * 1024 * 1024
        ),
    )(*(pltpu.with_memory_space_constraint(array, pltpu.HBM) for array in (eigvecs, reflectors.T, factors)))
    blocks = 8
    return pl.pallas_call(
        finish,
        out_shape=jax.ShapeDtypeStruct((rows, columns), F32),
        in_specs=[pl.BlockSpec(memory_space=pltpu.VMEM)] * 5,
        out_specs=pl.BlockSpec(memory_space=pltpu.HBM),
        scratch_shapes=[
            pltpu.VMEM((blocks, rows // blocks, columns), F32),
            pltpu.SemaphoreType.DMA((blocks,)),
        ],
        compiler_params=pltpu.CompilerParams(vmem_limit_bytes=32 * 1024 * 1024),
    )(*held)


def solution(mesh):
    return jax.shard_map(
        shards,
        mesh=mesh,
        in_specs=(P("prow", "pcol"), P("prow", "pcol"), P("pcol", None)),
        out_specs=P("prow", "pcol"),
        check_vma=False,
    )
```

```python
import functools

import jax
import jax.numpy as jnp
from jax import lax
from jax.experimental import pallas as pl
from jax.experimental.pallas import tpu as pltpu
from jax.sharding import PartitionSpec as P

MESH = pl.DeviceIdType.MESH
F32, BF16 = jnp.float32, jnp.bfloat16
PLANES = 8
ROWS = 32
CHIPS = 16
SLAB = 64
HALF = SLAB // 2
NN = (((1,), (0,)), ((), ()))
NT = (((1,), (1,)), ((), ()))
TN = (((0,), (0,)), ((), ()))
PARTS = (6, 4, 2, 2, 2)
LAST = len(PARTS) - 1
HEIGHTS = tuple(4 * pieces for pieces in PARTS)


def split(value):
    high = value.astype(BF16)
    return high, (value - high.astype(F32)).astype(BF16)


def product(left, right, dims):
    dot = functools.partial(lax.dot_general, dimension_numbers=dims, preferred_element_type=F32)
    return dot(left[0], right[0]) + (dot(left[1], right[0]) + dot(left[0], right[1]))


def stacked(left, right, dims):
    rows = left[0].shape[0]
    by_high = lax.dot_general(jnp.concatenate(left, axis=0), right[0], dims, preferred_element_type=F32)
    by_low = lax.dot_general(left[0], right[1], dims, preferred_element_type=F32)
    return by_high[:rows] + (by_high[rows:] + by_low)


def kernel(
    z_hbm, v_hbm, t_hbm, z_full, u_hi, u_lo, w_hi, w_lo,
    panel, v_hi, v_lo, z_hi, z_lo, z_sum, z_late, t_in, t_mine, t_planes, t_all, t_full,
    g_give, g_take, g_planes, g_all, g_pairs, gram, turned,
    local, ring_out, ring_in, crossing, spread, part_out, part_in, *buffers,
):
    z, p = lax.axis_index("pcol"), lax.axis_index("prow")
    chip, core = p // 2, lax.rem(p, 2)
    right, left = lax.rem(z + 1, PLANES), lax.rem(z + PLANES - 1, PLANES)
    twin = p + 1 - 2 * core
    count = len(PARTS)
    gives, takes, alls = (buffers[i * count : i * count + count] for i in range(3))
    mixes = buffers[3 * count :]

    def plane(offset):
        return lax.rem(z + offset, PLANES)

    ys, xs = ([lax.rem(at + offset, 4) for offset in range(4)] for at in (p // 8, chip))
    offsets = [(y, x) for y in (2, 1, 3, 0) for x in (2, 1, 3, 0)]
    offsets.sort(key=lambda at: -sum(min(step, 4 - step) for step in at))
    fellows = [(ys[y] * 4 + xs[x]) * 2 + core for y, x in offsets[:-1]]
    mates = [(ys[y] * 4 + xs[x]) * 2 + at for y, x in offsets for at in (1 - core, core)][:-1]

    barrier = pltpu.get_barrier_semaphore()
    for offset in (1, 7, 2, 6, 3, 5, 4):
        pl.semaphore_signal(barrier, inc=1, device_id={"pcol": plane(offset)}, device_id_type=MESH)

    for other in mates:
        pl.semaphore_signal(barrier, inc=1, device_id={"prow": other}, device_id_type=MESH)
    t_copy = pltpu.make_async_copy(t_hbm, t_in, local.at[0])
    own_copy = pltpu.make_async_copy(v_hbm, panel.at[z], local.at[1])
    z_copy = pltpu.make_async_copy(z_hbm, z_full, local.at[2])
    t_copy.start()
    own_copy.start()
    z_copy.start()
    pl.semaphore_wait(barrier, PLANES - 1 + ROWS - 1)

    def ring(way, step, half):
        rows = pl.ds(half * HALF, HALF)
        ref = panel.at[plane(PLANES - step) if way == 0 else plane(step), rows]
        return pltpu.make_async_remote_copy(
            v_hbm.at[rows] if step == 0 else ref, ref, ring_out.at[way, step, half], ring_in.at[way, step, half],
            device_id={"pcol": right if way == 0 else left}, device_id_type=MESH,
        )

    def take(step, turn):
        for way in range(2):
            ring(way, step, turn if way == 0 else 1 - turn).wait_recv()

    def give(step, turn):
        for way in range(2):
            half = turn if way == 0 else 1 - turn
            if step < 3 or half == way:
                ring(way, step, half).start()

    give(0, 0)

    t_copy.wait()
    for index in range(ROWS):
        row, lane = index // 4 * 8 + index % 2 * 4, index // 2 % 2 * 128
        t_mine[index] = t_in[row : row + 4, lane : lane + 128]
    t_planes[z] = t_mine[p]

    def from_planes(target, stage):
        ref = target.at[pl.ds(0, PLANES - 1)]
        return pltpu.make_async_remote_copy(
            ref, ref, crossing.at[0, stage], crossing.at[1, stage], device_id={"pcol": right}, device_id_type=MESH
        )

    def to_planes(target, stage):
        for offset in (4, 3, 5, 2, 6, 1, 7):
            pltpu.make_async_remote_copy(
                target.at[z], target.at[z], crossing.at[0, stage], crossing.at[1, stage],
                device_id={"pcol": plane(offset)}, device_id_type=MESH,
            ).start()

    to_planes(t_planes, 0)
    give(0, 1)

    def from_mates(target, stage):
        ref = target.at[pl.ds(0, ROWS - 1)]
        return pltpu.make_async_remote_copy(
            ref, ref, spread.at[0, stage], spread.at[1, stage], device_id={"pcol": right}, device_id_type=MESH
        )

    def to_mates(source, target, stage):
        for other in mates:
            pltpu.make_async_remote_copy(
                source(other), target.at[p], spread.at[0, stage], spread.at[1, stage],
                device_id={"prow": other}, device_id_type=MESH,
            ).start()
        target[p] = source(p)[...]

    def t_spread():
        from_planes(t_planes, 0).wait_recv()
        to_mates(lambda other: t_planes, t_all, 0)

    def t_collect():
        from_mates(t_all, 0).wait_recv()
        for index in range(ROWS):
            for slab in range(PLANES):
                row, lane = slab * SLAB + index // 4 * 8 + index % 2 * 4, index // 2 % 2 * 128
                t_full[row : row + 4, lane : lane + 128] = t_all[index, slab]

    def g_scatter():
        left_side, right_side = (
            tuple(jnp.concatenate([ref[slab] for slab in slabs], axis=0) for ref in (v_hi, v_lo))
            for slabs in ((z, behind[1]), (ahead[0], ahead[1]))
        )
        pairs = stacked(left_side, right_side, NT)
        for index in range(ROWS):
            g_give[index] = pairs[index * 4 : index * 4 + 4]
        to_mates(lambda other: g_give.at[other], g_take, 1)

    def g_gather():
        from_mates(g_take, 1).wait_recv()
        g_planes[z] = jnp.sum(g_take[...], axis=0)
        to_planes(g_planes, 1)

    def g_spread():
        from_planes(g_planes, 1).wait_recv()
        to_mates(lambda other: g_planes, g_all, 2)

    def g_collect():
        from_mates(g_all, 2).wait_recv()
        for index in range(ROWS):
            for w in range(PLANES):
                g_pairs[w, index * 4 : index * 4 + 4] = g_all[index, w]
        gram[...] = jnp.zeros_like(gram)
        for a in range(PLANES):
            for distance in range(1, 5):
                b = (a + distance) % PLANES
                if a // 4 == b // 4 or (distance == 4 and a > b):
                    continue
                w, row = (a, 0) if distance < 3 else ((a + 2) % PLANES, SLAB)
                lane = SLAB * (1 - distance % 2)
                gram[a * SLAB : a * SLAB + SLAB, b % 4 * SLAB : b % 4 * SLAB + SLAB] = g_pairs[
                    w, row : row + SLAB, lane : lane + SLAB
                ]

    def to_twin(part, stage, source, target):
        return pltpu.make_async_remote_copy(
            source, target, part_out.at[part, stage], part_in.at[part, stage],
            device_id={"prow": twin}, device_id_type=MESH,
        )

    def to_others(part, stage, source, target):
        for other in fellows if part < LAST else mates:
            pltpu.make_async_remote_copy(
                source(other // 2 if part < LAST else other), target, part_out.at[part, stage], part_in.at[part, stage],
                device_id={"prow": other}, device_id_type=MESH,
            ).start()

    def from_others(part, stage):
        ref = takes[part].at[pl.ds(0, takes[part].shape[0] - 1)]
        return pltpu.make_async_remote_copy(
            ref, ref, part_out.at[part, stage], part_in.at[part, stage],
            device_id={"prow": twin}, device_id_type=MESH,
        )

    def mix_copy(part):
        return to_twin(part, 0, gives[part].at[1 - core], mixes[part].at[0])

    def back_copy(part):
        return to_twin(part, 3, alls[part].at[core], alls[part].at[core])

    def scatter(part):
        source, target, me = gives[part], takes[part], chip if part < LAST else p
        if part < LAST:
            mix_copy(part).wait_recv()
            mixes[part][1] = source[core] + mixes[part][0]
            source = mixes[part].at[1]
        to_others(part, 1, lambda other: source.at[other], target.at[me])
        target[me] = source[me]

    def gather(part):
        from_others(part, 1).wait_recv()
        kept, me = (alls[part].at[core], chip) if part < LAST else (alls[part], p)
        kept[me] = jnp.sum(takes[part][...], axis=0)
        to_others(part, 2, lambda other: kept.at[me], kept.at[me])

    def give_back(part):
        from_others(part, 2).wait_recv()
        back_copy(part).start()

    def place(part, tile):
        return (tile % 2, tile // 2) if part < LAST else (tile,)

    def halves(slab, first=0, rows=SLAB):
        at = pl.ds(first, rows)
        v_hi[slab, at], v_lo[slab, at] = split(panel[slab, at])

    def sums_of(pieces):
        high, low = ([ref[slab, pl.ds(first, rows)] for slab, first, rows in pieces] for ref in (v_hi, v_lo))
        together = functools.partial(jnp.concatenate, axis=0)
        return stacked((together(high), together(low)), (z_hi[...], z_lo[...]), NN)

    def lay(part, sums):
        for index in range(PARTS[part] * 16):
            tile, slot = place(part, index % ROWS), index // ROWS * 8
            row, lane = index // 4 * 8, index % 4 * 128
            gives[part].at[*tile][slot : slot + 8] = sums[row : row + 8, lane : lane + 128]

    def landed(part):
        return back_copy(part) if part < LAST else from_others(part, 2)

    def collect(part, slabs):
        landed(part).wait_recv()
        for index in range(PARTS[part] * 16):
            tile, slot = place(part, index % ROWS), index // ROWS * 8
            slab, first = slabs[index // 16]
            row, lane = first + index % 16 // 4 * 8, index % 4 * 128
            z_sum[slab, row : row + 8, lane : lane + 128] = alls[part][*tile, slot : slot + 8]

    def collect_late(part, first):
        landed(part).wait_recv()
        for index in range(PARTS[part] * 16):
            tile, row, lane = place(part, index), first + index // 4 * 8, index % 4 * 128
            z_late[row : row + 8, lane : lane + 128] = alls[part][*tile]

    def both(slab):
        return [(slab, 0), (slab, HALF)]

    def compute(part, fresh, older=()):
        for piece in fresh:
            halves(*piece)
        lay(part, sums_of([*older, *fresh]))
        if part < LAST:
            mix_copy(part).start()

    behind = [plane(PLANES - 1 - step) for step in range(3)]
    ahead = [plane(1 + step) for step in range(3)]
    late = plane(4)
    z_sum[...] = jnp.zeros_like(z_sum)
    own_copy.wait()
    halves(z)
    z_copy.wait()
    z_hi[...], z_lo[...] = split(z_full[...])

    take(0, 0)
    give(1, 0)
    t_spread()
    take(0, 1)
    give(1, 1)
    compute(0, [(behind[0], 0, SLAB), (ahead[0], 0, SLAB)], [(z, 0, SLAB)])
    scatter(0)
    take(1, 0)
    give(2, 0)
    take(1, 1)
    give(2, 1)
    halves(behind[1])
    halves(ahead[1])
    g_scatter()
    compute(1, [], [(behind[1], 0, SLAB), (ahead[1], 0, SLAB)])
    gather(0)
    scatter(1)
    take(2, 0)
    g_gather()
    give(3, 0)
    compute(2, [(behind[2], 0, HALF), (ahead[2], HALF, HALF)])
    give_back(0)
    gather(1)
    scatter(2)
    take(2, 1)
    compute(3, [(behind[2], HALF, HALF), (ahead[2], 0, HALF)])
    g_spread()
    scatter(3)
    gather(2)
    give_back(1)
    collect(0, both(z) + both(behind[0]) + both(ahead[0]))
    t_collect()
    t_halves = split(t_full[...])
    take(3, 0)
    compute(4, [(late, 0, SLAB)])
    scatter(4)
    gather(3)
    collect(1, both(behind[1]) + both(ahead[1]))

    g_collect()
    upper, lower = slice(0, 4 * SLAB), slice(4 * SLAB, 8 * SLAB)
    first, second = (tuple(half[rows] for half in t_halves) for rows in (upper, lower))
    crossed = product(split(gram[upper] + gram[lower].T), second, NN)
    corner = -product(first, split(crossed), NN)
    none = jnp.zeros_like(corner)
    m = jnp.concatenate(
        [jnp.concatenate([t_full[upper], corner], axis=1), jnp.concatenate([none, t_full[lower]], axis=1)], axis=0
    )
    turned[...] = m.T.reshape(turned.shape)
    coeff = split(product(split(m), split(z_sum[...].reshape(PLANES * SLAB, -1)), NN))
    block = 256

    def take_off(first, last):
        for index in range(first, last):
            at = pl.ds(index * block, block)
            v = tuple(ref[:, :, at].reshape(PLANES * SLAB, block) for ref in (v_hi, v_lo))
            z_full[at] = z_full[at] - product(v, coeff, TN)

    take_off(0, 2)
    give_back(2)
    gather(4)
    pieces = [(behind[2], 0, HALF), (ahead[2], HALF, HALF), (behind[2], HALF, HALF), (ahead[2], 0, HALF), (late, 0, SLAB)]
    m_late = [turned[slab, pl.ds(start, rows)] for slab, start, rows in pieces]
    m_late = split(jnp.concatenate([*m_late, jnp.zeros_like(turned[0])], axis=0).T)
    take_off(2, 5)
    give_back(3)
    take_off(5, 8)
    for index in range(z_full.shape[0] // block):
        at = pl.ds(index * block, block)
        v = tuple(ref[:, :, at].reshape(PLANES * SLAB, block) for ref in (v_hi, v_lo))
        u_hi[at], u_lo[at] = split(product(v, m_late, TN))
    z_late[3 * SLAB :] = jnp.zeros_like(z_late[3 * SLAB :])
    collect_late(2, 0)
    collect_late(3, SLAB)
    collect_late(4, 2 * SLAB)
    w_hi[...], w_lo[...] = split(z_late[...])

    for step in range(4):
        for way in range(2):
            for half in range(2):
                if step < 3 or half == way:
                    ring(way, step, half).wait_send()
    from_mates(t_all, 0).wait_send()
    from_mates(g_take, 1).wait_send()
    from_mates(g_all, 2).wait_send()
    from_planes(t_planes, 0).wait_send()
    from_planes(g_planes, 1).wait_send()
    for part in range(count):
        from_others(part, 1).wait_send()
        from_others(part, 2).wait_send()
        if part < LAST:
            mix_copy(part).wait_send()
            back_copy(part).wait_send()


def finish(part, u_hi, u_lo, w_hi, w_lo, out, stage, sem):
    block = stage.shape[1]
    w = jnp.concatenate([w_hi[...], w_hi[...], w_lo[...]], axis=0)
    copies = []
    for index in range(stage.shape[0]):
        at = pl.ds(index * block, block)
        u = jnp.concatenate([u_hi[at], u_lo[at], u_hi[at]], axis=1)
        stage[index] = part[at] - lax.dot_general(u, w, NN, preferred_element_type=F32)
        copies.append(pltpu.make_async_copy(stage.at[index], out.at[at], sem.at[index]))
        copies[-1].start()
    for copy in copies:
        copy.wait()


def shards(eigvecs, reflectors, factors):
    rows, columns = eigvecs.shape
    width = PLANES * SLAB // 2
    scratch = [
        pltpu.VMEM((PLANES, SLAB, rows), F32),
        pltpu.VMEM((PLANES, SLAB, rows), BF16),
        pltpu.VMEM((PLANES, SLAB, rows), BF16),
        pltpu.VMEM((rows, columns), BF16),
        pltpu.VMEM((rows, columns), BF16),
        pltpu.VMEM((PLANES, SLAB, columns), F32),
        pltpu.VMEM((4 * SLAB, columns), F32),
        pltpu.VMEM((SLAB, width), F32),
        pltpu.VMEM((ROWS, 4, 128), F32),
        pltpu.VMEM((PLANES, 4, 128), F32),
        pltpu.VMEM((ROWS, PLANES, 4, 128), F32),
        pltpu.VMEM((PLANES * SLAB, width), F32),
        pltpu.VMEM((ROWS, 4, 128), F32),
        pltpu.VMEM((ROWS, 4, 128), F32),
        pltpu.VMEM((PLANES, 4, 128), F32),
        pltpu.VMEM((ROWS, PLANES, 4, 128), F32),
        pltpu.VMEM((PLANES, 2 * SLAB, 2 * SLAB), F32),
        pltpu.VMEM((PLANES * SLAB, width), F32),
        pltpu.VMEM((PLANES, SLAB, PLANES * SLAB), F32),
        pltpu.SemaphoreType.DMA((3,)),
        pltpu.SemaphoreType.DMA((2, 4, 2)),
        pltpu.SemaphoreType.DMA((2, 4, 2)),
        pltpu.SemaphoreType.DMA((2, 2)),
        pltpu.SemaphoreType.DMA((2, 3)),
        pltpu.SemaphoreType.DMA((len(PARTS), 4)),
        pltpu.SemaphoreType.DMA((len(PARTS), 4)),
    ]
    early, last = HEIGHTS[:-1], pltpu.VMEM((ROWS, HEIGHTS[-1], 128), F32)
    paired = [pltpu.VMEM((2, CHIPS, height, 128), F32) for height in early]
    single = [pltpu.VMEM((CHIPS, height, 128), F32) for height in early]
    scratch += [*paired, last, *single, last, *paired, last, *paired]
    held = pl.pallas_call(
        kernel,
        out_shape=[
            jax.ShapeDtypeStruct((rows, columns), F32),
            jax.ShapeDtypeStruct((rows, 4 * SLAB), BF16),
            jax.ShapeDtypeStruct((rows, 4 * SLAB), BF16),
            jax.ShapeDtypeStruct((4 * SLAB, columns), BF16),
            jax.ShapeDtypeStruct((4 * SLAB, columns), BF16),
        ],
        in_specs=[pl.BlockSpec(memory_space=pltpu.HBM)] * 3,
        out_specs=[pl.BlockSpec(memory_space=pltpu.VMEM)] * 5,
        scratch_shapes=scratch,
        compiler_params=pltpu.CompilerParams(
            collective_id=0, has_side_effects=True, vmem_limit_bytes=40 * 1024 * 1024
        ),
    )(*(pltpu.with_memory_space_constraint(array, pltpu.HBM) for array in (eigvecs, reflectors.T, factors)))
    blocks = 8
    return pl.pallas_call(
        finish,
        out_shape=jax.ShapeDtypeStruct((rows, columns), F32),
        in_specs=[pl.BlockSpec(memory_space=pltpu.VMEM)] * 5,
        out_specs=pl.BlockSpec(memory_space=pltpu.HBM),
        scratch_shapes=[
            pltpu.VMEM((blocks, rows // blocks, columns), F32),
            pltpu.SemaphoreType.DMA((blocks,)),
        ],
        compiler_params=pltpu.CompilerParams(vmem_limit_bytes=32 * 1024 * 1024),
    )(*held)


def solution(mesh):
    return jax.shard_map(
        shards,
        mesh=mesh,
        in_specs=(P("prow", "pcol"), P("prow", "pcol"), P("pcol", None)),
        out_specs=P("prow", "pcol"),
        check_vma=False,
    )
```

```python
import functools

import jax
import jax.numpy as jnp
from jax import lax
from jax.experimental import pallas as pl
from jax.experimental.pallas import tpu as pltpu
from jax.sharding import PartitionSpec as P

MESH = pl.DeviceIdType.MESH
F32, BF16 = jnp.float32, jnp.bfloat16
PLANES = 8
ROWS = 32
CHIPS = 16
SLAB = 64
HALF = SLAB // 2
NN = (((1,), (0,)), ((), ()))
NT = (((1,), (1,)), ((), ()))
TN = (((0,), (0,)), ((), ()))
PARTS = (6, 4, 2, 2, 2)
LAST = len(PARTS) - 1
HEIGHTS = tuple(4 * pieces for pieces in PARTS)


def split(value):
    high = value.astype(BF16)
    return high, (value - high.astype(F32)).astype(BF16)


def product(left, right, dims):
    dot = functools.partial(lax.dot_general, dimension_numbers=dims, preferred_element_type=F32)
    return dot(left[0], right[0]) + (dot(left[1], right[0]) + dot(left[0], right[1]))


def stacked(left, right, dims):
    rows = left[0].shape[0]
    by_high = lax.dot_general(jnp.concatenate(left, axis=0), right[0], dims, preferred_element_type=F32)
    by_low = lax.dot_general(left[0], right[1], dims, preferred_element_type=F32)
    return by_high[:rows] + (by_high[rows:] + by_low)


def kernel(
    z_hbm, v_hbm, t_hbm, z_full, u_hi, u_lo, w_hi, w_lo,
    panel, v_hi, v_lo, z_hi, z_lo, z_sum, z_late, t_in, t_mine, t_planes, t_all, t_full,
    g_give, g_take, g_planes, g_all, g_pairs, gram, turned,
    local, ring_out, ring_in, crossing, spread, part_out, part_in, *buffers,
):
    z, p = lax.axis_index("pcol"), lax.axis_index("prow")
    chip, core = p // 2, lax.rem(p, 2)
    right, left = lax.rem(z + 1, PLANES), lax.rem(z + PLANES - 1, PLANES)
    twin = p + 1 - 2 * core
    count = len(PARTS)
    gives, takes, alls = (buffers[i * count : i * count + count] for i in range(3))
    mixes = buffers[3 * count :]

    def plane(offset):
        return lax.rem(z + offset, PLANES)

    ys, xs = ([lax.rem(at + offset, 4) for offset in range(4)] for at in (p // 8, chip))
    offsets = [(y, x) for y in (2, 1, 3, 0) for x in (2, 1, 3, 0)]
    offsets.sort(key=lambda at: -sum(min(step, 4 - step) for step in at))
    fellows = [(ys[y] * 4 + xs[x]) * 2 + core for y, x in offsets[:-1]]
    mates = [(ys[y] * 4 + xs[x]) * 2 + at for y, x in offsets for at in (1 - core, core)][:-1]

    barrier = pltpu.get_barrier_semaphore()
    for offset in (1, 7, 2, 6, 3, 5, 4):
        pl.semaphore_signal(barrier, inc=1, device_id={"pcol": plane(offset)}, device_id_type=MESH)

    for other in mates:
        pl.semaphore_signal(barrier, inc=1, device_id={"prow": other}, device_id_type=MESH)
    t_copy = pltpu.make_async_copy(t_hbm, t_in, local.at[0])
    own_copy = pltpu.make_async_copy(v_hbm, panel.at[z], local.at[1])
    z_copy = pltpu.make_async_copy(z_hbm, z_full, local.at[2])
    t_copy.start()
    own_copy.start()
    z_copy.start()
    pl.semaphore_wait(barrier, PLANES - 1 + ROWS - 1)

    def ring(way, step, half):
        rows = pl.ds(half * HALF, HALF)
        ref = panel.at[plane(PLANES - step) if way == 0 else plane(step), rows]
        return pltpu.make_async_remote_copy(
            v_hbm.at[rows] if step == 0 else ref, ref, ring_out.at[way, step, half], ring_in.at[way, step, half],
            device_id={"pcol": right if way == 0 else left}, device_id_type=MESH,
        )

    def take(step, turn):
        for way in range(2):
            ring(way, step, turn if way == 0 else 1 - turn).wait_recv()

    def give(step, turn):
        for way in range(2):
            half = turn if way == 0 else 1 - turn
            if step < 3 or half == way:
                ring(way, step, half).start()

    give(0, 0)

    t_copy.wait()
    for index in range(ROWS):
        row, lane = index // 4 * 8 + index % 2 * 4, index // 2 % 2 * 128
        t_mine[index] = t_in[row : row + 4, lane : lane + 128]
    t_planes[z] = t_mine[p]

    def from_planes(target, stage):
        ref = target.at[pl.ds(0, PLANES - 1)]
        return pltpu.make_async_remote_copy(
            ref, ref, crossing.at[0, stage], crossing.at[1, stage], device_id={"pcol": right}, device_id_type=MESH
        )

    def to_planes(target, stage):
        for offset in (4, 3, 5, 2, 6, 1, 7):
            pltpu.make_async_remote_copy(
                target.at[z], target.at[z], crossing.at[0, stage], crossing.at[1, stage],
                device_id={"pcol": plane(offset)}, device_id_type=MESH,
            ).start()

    to_planes(t_planes, 0)
    give(0, 1)

    def from_mates(target, stage):
        ref = target.at[pl.ds(0, ROWS - 1)]
        return pltpu.make_async_remote_copy(
            ref, ref, spread.at[0, stage], spread.at[1, stage], device_id={"pcol": right}, device_id_type=MESH
        )

    def to_mates(source, target, stage):
        for other in mates:
            pltpu.make_async_remote_copy(
                source(other), target.at[p], spread.at[0, stage], spread.at[1, stage],
                device_id={"prow": other}, device_id_type=MESH,
            ).start()
        target[p] = source(p)[...]

    def t_spread():
        from_planes(t_planes, 0).wait_recv()
        to_mates(lambda other: t_planes, t_all, 0)

    def t_collect():
        from_mates(t_all, 0).wait_recv()
        for index in range(ROWS):
            for slab in range(PLANES):
                row, lane = slab * SLAB + index // 4 * 8 + index % 2 * 4, index // 2 % 2 * 128
                t_full[row : row + 4, lane : lane + 128] = t_all[index, slab]

    def g_scatter():
        left_side, right_side = (
            tuple(jnp.concatenate([ref[slab] for slab in slabs], axis=0) for ref in (v_hi, v_lo))
            for slabs in ((z, behind[1]), (ahead[0], ahead[1]))
        )
        pairs = stacked(left_side, right_side, NT)
        for index in range(ROWS):
            g_give[index] = pairs[index * 4 : index * 4 + 4]
        to_mates(lambda other: g_give.at[other], g_take, 1)

    def g_gather():
        from_mates(g_take, 1).wait_recv()
        g_planes[z] = jnp.sum(g_take[...], axis=0)
        to_planes(g_planes, 1)

    def g_spread():
        from_planes(g_planes, 1).wait_recv()
        to_mates(lambda other: g_planes, g_all, 2)

    def g_collect():
        from_mates(g_all, 2).wait_recv()
        for index in range(ROWS):
            for w in range(PLANES):
                g_pairs[w, index * 4 : index * 4 + 4] = g_all[index, w]
        gram[...] = jnp.zeros_like(gram)
        for a in range(PLANES):
            for distance in range(1, 5):
                b = (a + distance) % PLANES
                if a // 4 == b // 4 or (distance == 4 and a > b):
                    continue
                w, row = (a, 0) if distance < 3 else ((a + 2) % PLANES, SLAB)
                lane = SLAB * (1 - distance % 2)
                gram[a * SLAB : a * SLAB + SLAB, b % 4 * SLAB : b % 4 * SLAB + SLAB] = g_pairs[
                    w, row : row + SLAB, lane : lane + SLAB
                ]

    def to_twin(part, stage, source, target):
        return pltpu.make_async_remote_copy(
            source, target, part_out.at[part, stage], part_in.at[part, stage],
            device_id={"prow": twin}, device_id_type=MESH,
        )

    def to_others(part, stage, source, target):
        for other in fellows if part < LAST else mates:
            pltpu.make_async_remote_copy(
                source(other // 2 if part < LAST else other), target, part_out.at[part, stage], part_in.at[part, stage],
                device_id={"prow": other}, device_id_type=MESH,
            ).start()

    def from_others(part, stage):
        ref = takes[part].at[pl.ds(0, takes[part].shape[0] - 1)]
        return pltpu.make_async_remote_copy(
            ref, ref, part_out.at[part, stage], part_in.at[part, stage],
            device_id={"prow": twin}, device_id_type=MESH,
        )

    def mix_copy(part):
        return to_twin(part, 0, gives[part].at[1 - core], mixes[part].at[0])

    def back_copy(part):
        return to_twin(part, 3, alls[part].at[core], alls[part].at[core])

    def scatter(part):
        source, target, me = gives[part], takes[part], chip if part < LAST else p
        if part < LAST:
            mix_copy(part).wait_recv()
            mixes[part][1] = source[core] + mixes[part][0]
            source = mixes[part].at[1]
        to_others(part, 1, lambda other: source.at[other], target.at[me])
        target[me] = source[me]

    def gather(part):
        from_others(part, 1).wait_recv()
        kept, me = (alls[part].at[core], chip) if part < LAST else (alls[part], p)
        kept[me] = jnp.sum(takes[part][...], axis=0)
        to_others(part, 2, lambda other: kept.at[me], kept.at[me])

    def give_back(part):
        from_others(part, 2).wait_recv()
        back_copy(part).start()

    def place(part, tile):
        return (tile % 2, tile // 2) if part < LAST else (tile,)

    def halves(slab, first=0, rows=SLAB):
        at = pl.ds(first, rows)
        v_hi[slab, at], v_lo[slab, at] = split(panel[slab, at])

    def sums_of(pieces):
        high, low = ([ref[slab, pl.ds(first, rows)] for slab, first, rows in pieces] for ref in (v_hi, v_lo))
        together = functools.partial(jnp.concatenate, axis=0)
        return stacked((together(high), together(low)), (z_hi[...], z_lo[...]), NN)

    def lay(part, sums):
        for index in range(PARTS[part] * 16):
            tile, slot = place(part, index % ROWS), index // ROWS * 8
            row, lane = index // 4 * 8, index % 4 * 128
            gives[part].at[*tile][slot : slot + 8] = sums[row : row + 8, lane : lane + 128]

    def landed(part):
        return back_copy(part) if part < LAST else from_others(part, 2)

    def collect(part, slabs):
        landed(part).wait_recv()
        for index in range(PARTS[part] * 16):
            tile, slot = place(part, index % ROWS), index // ROWS * 8
            slab, first = slabs[index // 16]
            row, lane = first + index % 16 // 4 * 8, index % 4 * 128
            z_sum[slab, row : row + 8, lane : lane + 128] = alls[part][*tile, slot : slot + 8]

    def collect_late(part, first):
        landed(part).wait_recv()
        for index in range(PARTS[part] * 16):
            tile, row, lane = place(part, index), first + index // 4 * 8, index % 4 * 128
            z_late[row : row + 8, lane : lane + 128] = alls[part][*tile]

    def both(slab):
        return [(slab, 0), (slab, HALF)]

    def compute(part, fresh, older=()):
        for piece in fresh:
            halves(*piece)
        lay(part, sums_of([*older, *fresh]))
        if part < LAST:
            mix_copy(part).start()

    behind = [plane(PLANES - 1 - step) for step in range(3)]
    ahead = [plane(1 + step) for step in range(3)]
    late = plane(4)
    z_sum[...] = jnp.zeros_like(z_sum)
    own_copy.wait()
    halves(z)
    z_copy.wait()
    z_hi[...], z_lo[...] = split(z_full[...])

    take(0, 0)
    give(1, 0)
    t_spread()
    take(0, 1)
    give(1, 1)
    compute(0, [(behind[0], 0, SLAB), (ahead[0], 0, SLAB)], [(z, 0, SLAB)])
    scatter(0)
    take(1, 0)
    give(2, 0)
    take(1, 1)
    give(2, 1)
    halves(behind[1])
    halves(ahead[1])
    g_scatter()
    compute(1, [], [(behind[1], 0, SLAB), (ahead[1], 0, SLAB)])
    gather(0)
    scatter(1)
    take(2, 0)
    g_gather()
    give(3, 0)
    compute(2, [(behind[2], 0, HALF), (ahead[2], HALF, HALF)])
    give_back(0)
    gather(1)
    scatter(2)
    take(2, 1)
    compute(3, [(behind[2], HALF, HALF), (ahead[2], 0, HALF)])
    g_spread()
    scatter(3)
    gather(2)
    give_back(1)
    collect(0, both(z) + both(behind[0]) + both(ahead[0]))
    t_collect()
    t_halves = split(t_full[...])
    take(3, 0)
    compute(4, [(late, 0, SLAB)])
    scatter(4)
    gather(3)
    collect(1, both(behind[1]) + both(ahead[1]))

    g_collect()
    upper, lower = slice(0, 4 * SLAB), slice(4 * SLAB, 8 * SLAB)
    first, second = (tuple(half[rows] for half in t_halves) for rows in (upper, lower))
    crossed = product(split(gram[upper] + gram[lower].T), second, NN)
    corner = -product(first, split(crossed), NN)
    none = jnp.zeros_like(corner)
    m = jnp.concatenate(
        [jnp.concatenate([t_full[upper], corner], axis=1), jnp.concatenate([none, t_full[lower]], axis=1)], axis=0
    )
    turned[...] = m.T.reshape(turned.shape)
    coeff = split(product(split(m), split(z_sum[...].reshape(PLANES * SLAB, -1)), NN))
    pieces = [(behind[2], 0, HALF), (ahead[2], HALF, HALF), (behind[2], HALF, HALF), (ahead[2], 0, HALF), (late, 0, SLAB)]
    m_late = [turned[slab, pl.ds(start, rows)] for slab, start, rows in pieces]
    m_late = split(jnp.concatenate([*m_late, jnp.zeros_like(turned[0])], axis=0).T)
    sides = tuple(jnp.concatenate(both_sides, axis=1) for both_sides in zip(coeff, m_late))
    block, columns = 256, z_full.shape[1]

    def take_off(first, last):
        for index in range(first, last):
            at = pl.ds(index * block, block)
            v = tuple(ref[:, :, at].reshape(PLANES * SLAB, block) for ref in (v_hi, v_lo))
            share = product(v, sides, TN)
            z_full[at] = z_full[at] - share[:, :columns]
            u_hi[at], u_lo[at] = split(share[:, columns:])

    give_back(2)
    gather(4)
    take_off(0, 4)
    give_back(3)
    take_off(4, 8)
    z_late[3 * SLAB :] = jnp.zeros_like(z_late[3 * SLAB :])
    collect_late(2, 0)
    collect_late(3, SLAB)

    for step in range(4):
        for way in range(2):
            for half in range(2):
                if step < 3 or half == way:
                    ring(way, step, half).wait_send()
    from_mates(t_all, 0).wait_send()
    from_mates(g_take, 1).wait_send()
    from_mates(g_all, 2).wait_send()
    from_planes(t_planes, 0).wait_send()
    from_planes(g_planes, 1).wait_send()
    for part in range(count):
        from_others(part, 1).wait_send()
        from_others(part, 2).wait_send()
        if part < LAST:
            mix_copy(part).wait_send()
            back_copy(part).wait_send()
    collect_late(4, 2 * SLAB)
    w_hi[...], w_lo[...] = split(z_late[...])


def finish(part, u_hi, u_lo, w_hi, w_lo, out, stage, sem):
    block = stage.shape[1]
    w = jnp.concatenate([w_hi[...], w_hi[...], w_lo[...]], axis=0)
    copies = []
    for index in range(stage.shape[0]):
        at = pl.ds(index * block, block)
        u = jnp.concatenate([u_hi[at], u_lo[at], u_hi[at]], axis=1)
        stage[index] = part[at] - lax.dot_general(u, w, NN, preferred_element_type=F32)
        copies.append(pltpu.make_async_copy(stage.at[index], out.at[at], sem.at[index]))
        copies[-1].start()
    for copy in copies:
        copy.wait()


def shards(eigvecs, reflectors, factors):
    rows, columns = eigvecs.shape
    width = PLANES * SLAB // 2
    scratch = [
        pltpu.VMEM((PLANES, SLAB, rows), F32),
        pltpu.VMEM((PLANES, SLAB, rows), BF16),
        pltpu.VMEM((PLANES, SLAB, rows), BF16),
        pltpu.VMEM((rows, columns), BF16),
        pltpu.VMEM((rows, columns), BF16),
        pltpu.VMEM((PLANES, SLAB, columns), F32),
        pltpu.VMEM((4 * SLAB, columns), F32),
        pltpu.VMEM((SLAB, width), F32),
        pltpu.VMEM((ROWS, 4, 128), F32),
        pltpu.VMEM((PLANES, 4, 128), F32),
        pltpu.VMEM((ROWS, PLANES, 4, 128), F32),
        pltpu.VMEM((PLANES * SLAB, width), F32),
        pltpu.VMEM((ROWS, 4, 128), F32),
        pltpu.VMEM((ROWS, 4, 128), F32),
        pltpu.VMEM((PLANES, 4, 128), F32),
        pltpu.VMEM((ROWS, PLANES, 4, 128), F32),
        pltpu.VMEM((PLANES, 2 * SLAB, 2 * SLAB), F32),
        pltpu.VMEM((PLANES * SLAB, width), F32),
        pltpu.VMEM((PLANES, SLAB, PLANES * SLAB), F32),
        pltpu.SemaphoreType.DMA((3,)),
        pltpu.SemaphoreType.DMA((2, 4, 2)),
        pltpu.SemaphoreType.DMA((2, 4, 2)),
        pltpu.SemaphoreType.DMA((2, 2)),
        pltpu.SemaphoreType.DMA((2, 3)),
        pltpu.SemaphoreType.DMA((len(PARTS), 4)),
        pltpu.SemaphoreType.DMA((len(PARTS), 4)),
    ]
    early, last = HEIGHTS[:-1], pltpu.VMEM((ROWS, HEIGHTS[-1], 128), F32)
    paired = [pltpu.VMEM((2, CHIPS, height, 128), F32) for height in early]
    single = [pltpu.VMEM((CHIPS, height, 128), F32) for height in early]
    scratch += [*paired, last, *single, last, *paired, last, *paired]
    held = pl.pallas_call(
        kernel,
        out_shape=[
            jax.ShapeDtypeStruct((rows, columns), F32),
            jax.ShapeDtypeStruct((rows, 4 * SLAB), BF16),
            jax.ShapeDtypeStruct((rows, 4 * SLAB), BF16),
            jax.ShapeDtypeStruct((4 * SLAB, columns), BF16),
            jax.ShapeDtypeStruct((4 * SLAB, columns), BF16),
        ],
        in_specs=[pl.BlockSpec(memory_space=pltpu.HBM)] * 3,
        out_specs=[pl.BlockSpec(memory_space=pltpu.VMEM)] * 5,
        scratch_shapes=scratch,
        compiler_params=pltpu.CompilerParams(
            collective_id=0, has_side_effects=True, vmem_limit_bytes=40 * 1024 * 1024
        ),
    )(*(pltpu.with_memory_space_constraint(array, pltpu.HBM) for array in (eigvecs, reflectors.T, factors)))
    blocks = 8
    return pl.pallas_call(
        finish,
        out_shape=jax.ShapeDtypeStruct((rows, columns), F32),
        in_specs=[pl.BlockSpec(memory_space=pltpu.VMEM)] * 5,
        out_specs=pl.BlockSpec(memory_space=pltpu.HBM),
        scratch_shapes=[
            pltpu.VMEM((blocks, rows // blocks, columns), F32),
            pltpu.SemaphoreType.DMA((blocks,)),
        ],
        compiler_params=pltpu.CompilerParams(vmem_limit_bytes=32 * 1024 * 1024),
    )(*held)


def solution(mesh):
    return jax.shard_map(
        shards,
        mesh=mesh,
        in_specs=(P("prow", "pcol"), P("prow", "pcol"), P("pcol", None)),
        out_specs=P("prow", "pcol"),
        check_vma=False,
    )
```

```python
import functools

import jax
import jax.numpy as jnp
from jax import lax
from jax.experimental import pallas as pl
from jax.experimental.pallas import tpu as pltpu
from jax.sharding import PartitionSpec as P

MESH = pl.DeviceIdType.MESH
F32, BF16 = jnp.float32, jnp.bfloat16
PLANES = 8
ROWS = 32
CHIPS = 16
SLAB = 64
HALF = SLAB // 2
NN = (((1,), (0,)), ((), ()))
NT = (((1,), (1,)), ((), ()))
TN = (((0,), (0,)), ((), ()))
PARTS = (6, 4, 2, 2, 2)
LAST = len(PARTS) - 1
HEIGHTS = tuple(4 * pieces for pieces in PARTS)


def split(value):
    high = value.astype(BF16)
    return high, (value - high.astype(F32)).astype(BF16)


def product(left, right, dims):
    dot = functools.partial(lax.dot_general, dimension_numbers=dims, preferred_element_type=F32)
    return dot(left[0], right[0]) + (dot(left[1], right[0]) + dot(left[0], right[1]))


def stacked(left, right, dims):
    rows = left[0].shape[0]
    by_high = lax.dot_general(jnp.concatenate(left, axis=0), right[0], dims, preferred_element_type=F32)
    by_low = lax.dot_general(left[0], right[1], dims, preferred_element_type=F32)
    return by_high[:rows] + (by_high[rows:] + by_low)


def kernel(
    z_hbm, v_hbm, t_hbm, z_full, u_hi, u_lo, w_hi, w_lo,
    panel, v_hi, v_lo, z_hi, z_lo, z_sum, z_late, t_in, t_mine, t_planes, t_all, t_full,
    g_give, g_take, g_planes, g_all, g_pairs, gram, turned,
    local, ring_out, ring_in, crossing, spread, part_out, part_in, *buffers,
):
    z, p = lax.axis_index("pcol"), lax.axis_index("prow")
    chip, core = p // 2, lax.rem(p, 2)
    right, left = lax.rem(z + 1, PLANES), lax.rem(z + PLANES - 1, PLANES)
    twin = p + 1 - 2 * core
    count = len(PARTS)
    gives, takes, alls = (buffers[i * count : i * count + count] for i in range(3))
    mixes = buffers[3 * count :]

    def plane(offset):
        return lax.rem(z + offset, PLANES)

    ys, xs = ([lax.rem(at + offset, 4) for offset in range(4)] for at in (p // 8, chip))
    offsets = [(y, x) for y in (2, 1, 3, 0) for x in (2, 1, 3, 0)]
    offsets.sort(key=lambda at: -sum(min(step, 4 - step) for step in at))
    fellows = [(ys[y] * 4 + xs[x]) * 2 + core for y, x in offsets[:-1]]
    mates = [(ys[y] * 4 + xs[x]) * 2 + at for y, x in offsets for at in (1 - core, core)][:-1]

    barrier = pltpu.get_barrier_semaphore()
    for offset in (1, 7, 2, 6, 3, 5, 4):
        pl.semaphore_signal(barrier, inc=1, device_id={"pcol": plane(offset)}, device_id_type=MESH)

    for other in mates:
        pl.semaphore_signal(barrier, inc=1, device_id={"prow": other}, device_id_type=MESH)
    t_copy = pltpu.make_async_copy(t_hbm, t_in, local.at[0])
    own_copy = pltpu.make_async_copy(v_hbm, panel.at[z], local.at[1])
    z_copy = pltpu.make_async_copy(z_hbm, z_full, local.at[2])
    t_copy.start()
    own_copy.start()
    z_copy.start()
    pl.semaphore_wait(barrier, PLANES - 1 + ROWS - 1)

    def ring(way, step, half):
        rows = pl.ds(half * HALF, HALF)
        ref = panel.at[plane(PLANES - step) if way == 0 else plane(step), rows]
        return pltpu.make_async_remote_copy(
            v_hbm.at[rows] if step == 0 else ref, ref, ring_out.at[way, step, half], ring_in.at[way, step, half],
            device_id={"pcol": right if way == 0 else left}, device_id_type=MESH,
        )

    def take(step, turn):
        for way in range(2):
            ring(way, step, turn if way == 0 else 1 - turn).wait_recv()

    def give(step, turn):
        for way in range(2):
            half = turn if way == 0 else 1 - turn
            if step < 3 or half == way:
                ring(way, step, half).start()

    give(0, 0)

    t_copy.wait()
    for index in range(ROWS):
        row, lane = index // 4 * 8 + index % 2 * 4, index // 2 % 2 * 128
        t_mine[index] = t_in[row : row + 4, lane : lane + 128]
    t_planes[z] = t_mine[p]

    def from_planes(target, stage):
        ref = target.at[pl.ds(0, PLANES - 1)]
        return pltpu.make_async_remote_copy(
            ref, ref, crossing.at[0, stage], crossing.at[1, stage], device_id={"pcol": right}, device_id_type=MESH
        )

    def to_planes(target, stage):
        for offset in (4, 3, 5, 2, 6, 1, 7):
            pltpu.make_async_remote_copy(
                target.at[z], target.at[z], crossing.at[0, stage], crossing.at[1, stage],
                device_id={"pcol": plane(offset)}, device_id_type=MESH,
            ).start()

    to_planes(t_planes, 0)
    give(0, 1)

    def from_mates(target, stage):
        ref = target.at[pl.ds(0, ROWS - 1)]
        return pltpu.make_async_remote_copy(
            ref, ref, spread.at[0, stage], spread.at[1, stage], device_id={"pcol": right}, device_id_type=MESH
        )

    def to_mates(source, target, stage):
        for other in mates:
            pltpu.make_async_remote_copy(
                source(other), target.at[p], spread.at[0, stage], spread.at[1, stage],
                device_id={"prow": other}, device_id_type=MESH,
            ).start()
        target[p] = source(p)[...]

    def t_spread():
        from_planes(t_planes, 0).wait_recv()
        to_mates(lambda other: t_planes, t_all, 0)

    def t_collect():
        from_mates(t_all, 0).wait_recv()
        for index in range(ROWS):
            for slab in range(PLANES):
                row, lane = slab * SLAB + index // 4 * 8 + index % 2 * 4, index // 2 % 2 * 128
                t_full[row : row + 4, lane : lane + 128] = t_all[index, slab]

    def g_scatter():
        left_side, right_side = (
            tuple(jnp.concatenate([ref[slab] for slab in slabs], axis=0) for ref in (v_hi, v_lo))
            for slabs in ((z, behind[1]), (ahead[0], ahead[1]))
        )
        pairs = stacked(left_side, right_side, NT)
        for index in range(ROWS):
            g_give[index] = pairs[index * 4 : index * 4 + 4]
        to_mates(lambda other: g_give.at[other], g_take, 1)

    def g_gather():
        from_mates(g_take, 1).wait_recv()
        g_planes[z] = jnp.sum(g_take[...], axis=0)
        to_planes(g_planes, 1)

    def g_spread():
        from_planes(g_planes, 1).wait_recv()
        to_mates(lambda other: g_planes, g_all, 2)

    def g_collect():
        from_mates(g_all, 2).wait_recv()
        for index in range(ROWS):
            for w in range(PLANES):
                g_pairs[w, index * 4 : index * 4 + 4] = g_all[index, w]
        gram[...] = jnp.zeros_like(gram)
        for a in range(PLANES):
            for distance in range(1, 5):
                b = (a + distance) % PLANES
                if a // 4 == b // 4 or (distance == 4 and a > b):
                    continue
                w, row = (a, 0) if distance < 3 else ((a + 2) % PLANES, SLAB)
                lane = SLAB * (1 - distance % 2)
                gram[a * SLAB : a * SLAB + SLAB, b % 4 * SLAB : b % 4 * SLAB + SLAB] = g_pairs[
                    w, row : row + SLAB, lane : lane + SLAB
                ]

    def to_twin(part, stage, source, target):
        return pltpu.make_async_remote_copy(
            source, target, part_out.at[part, stage], part_in.at[part, stage],
            device_id={"prow": twin}, device_id_type=MESH,
        )

    def to_others(part, stage, source, target):
        for other in fellows if part < LAST else mates:
            pltpu.make_async_remote_copy(
                source(other // 2 if part < LAST else other), target, part_out.at[part, stage], part_in.at[part, stage],
                device_id={"prow": other}, device_id_type=MESH,
            ).start()

    def from_others(part, stage):
        ref = takes[part].at[pl.ds(0, takes[part].shape[0] - 1)]
        return pltpu.make_async_remote_copy(
            ref, ref, part_out.at[part, stage], part_in.at[part, stage],
            device_id={"prow": twin}, device_id_type=MESH,
        )

    def mix_copy(part):
        return to_twin(part, 0, gives[part].at[1 - core], mixes[part].at[0])

    def back_copy(part):
        return to_twin(part, 3, alls[part].at[core], alls[part].at[core])

    def scatter(part):
        source, target, me = gives[part], takes[part], chip if part < LAST else p
        if part < LAST:
            mix_copy(part).wait_recv()
            mixes[part][1] = source[core] + mixes[part][0]
            source = mixes[part].at[1]
        to_others(part, 1, lambda other: source.at[other], target.at[me])
        target[me] = source[me]

    def gather(part):
        from_others(part, 1).wait_recv()
        kept, me = (alls[part].at[core], chip) if part < LAST else (alls[part], p)
        kept[me] = jnp.sum(takes[part][...], axis=0)
        to_others(part, 2, lambda other: kept.at[me], kept.at[me])

    def give_back(part):
        from_others(part, 2).wait_recv()
        back_copy(part).start()

    def place(part, tile):
        return (tile % 2, tile // 2) if part < LAST else (tile,)

    def halves(slab, first=0, rows=SLAB):
        at = pl.ds(first, rows)
        v_hi[slab, at], v_lo[slab, at] = split(panel[slab, at])

    def sums_of(pieces):
        high, low = ([ref[slab, pl.ds(first, rows)] for slab, first, rows in pieces] for ref in (v_hi, v_lo))
        together = functools.partial(jnp.concatenate, axis=0)
        return stacked((together(high), together(low)), (z_hi[...], z_lo[...]), NN)

    def lay(part, sums):
        for index in range(PARTS[part] * 16):
            tile, slot = place(part, index % ROWS), index // ROWS * 8
            row, lane = index // 4 * 8, index % 4 * 128
            gives[part].at[*tile][slot : slot + 8] = sums[row : row + 8, lane : lane + 128]

    def landed(part):
        return back_copy(part) if part < LAST else from_others(part, 2)

    def collect(part, slabs):
        landed(part).wait_recv()
        for index in range(PARTS[part] * 16):
            tile, slot = place(part, index % ROWS), index // ROWS * 8
            slab, first = slabs[index // 16]
            row, lane = first + index % 16 // 4 * 8, index % 4 * 128
            z_sum[slab, row : row + 8, lane : lane + 128] = alls[part][*tile, slot : slot + 8]

    def collect_late(part, first):
        landed(part).wait_recv()
        for index in range(PARTS[part] * 16):
            tile, row, lane = place(part, index), first + index // 4 * 8, index % 4 * 128
            z_late[row : row + 8, lane : lane + 128] = alls[part][*tile]

    def both(slab):
        return [(slab, 0), (slab, HALF)]

    def compute(part, fresh, older=()):
        for piece in fresh:
            halves(*piece)
        lay(part, sums_of([*older, *fresh]))
        if part < LAST:
            mix_copy(part).start()

    behind = [plane(PLANES - 1 - step) for step in range(3)]
    ahead = [plane(1 + step) for step in range(3)]
    late = plane(4)
    z_sum[...] = jnp.zeros_like(z_sum)
    own_copy.wait()
    halves(z)
    z_copy.wait()
    z_hi[...], z_lo[...] = split(z_full[...])

    take(0, 0)
    give(1, 0)
    t_spread()
    take(0, 1)
    give(1, 1)
    compute(0, [(behind[0], 0, SLAB), (ahead[0], 0, SLAB)], [(z, 0, SLAB)])
    scatter(0)
    take(1, 0)
    give(2, 0)
    take(1, 1)
    give(2, 1)
    halves(behind[1])
    halves(ahead[1])
    g_scatter()
    compute(1, [], [(behind[1], 0, SLAB), (ahead[1], 0, SLAB)])
    gather(0)
    scatter(1)
    take(2, 0)
    g_gather()
    give(3, 0)
    compute(2, [(behind[2], 0, HALF), (ahead[2], HALF, HALF)])
    give_back(0)
    gather(1)
    scatter(2)
    take(2, 1)
    compute(3, [(behind[2], HALF, HALF), (ahead[2], 0, HALF)])
    g_spread()
    scatter(3)
    gather(2)
    give_back(1)
    collect(0, both(z) + both(behind[0]) + both(ahead[0]))
    t_collect()
    t_halves = split(t_full[...])
    take(3, 0)
    compute(4, [(late, 0, SLAB)])
    scatter(4)
    gather(3)
    collect(1, both(behind[1]) + both(ahead[1]))

    g_collect()
    upper, lower = slice(0, 4 * SLAB), slice(4 * SLAB, 8 * SLAB)
    first, second = (tuple(half[rows] for half in t_halves) for rows in (upper, lower))
    crossed = product(split(gram[upper] + gram[lower].T), second, NN)
    corner = -product(first, split(crossed), NN)
    none = jnp.zeros_like(corner)
    m = jnp.concatenate(
        [jnp.concatenate([t_full[upper], corner], axis=1), jnp.concatenate([none, t_full[lower]], axis=1)], axis=0
    )
    turned[...] = m.T.reshape(turned.shape)
    coeff = split(product(split(m), split(z_sum[...].reshape(PLANES * SLAB, -1)), NN))
    pieces = [(behind[2], 0, HALF), (ahead[2], HALF, HALF), (behind[2], HALF, HALF), (ahead[2], 0, HALF), (late, 0, SLAB)]
    m_late = [turned[slab, pl.ds(start, rows)] for slab, start, rows in pieces]
    m_late = split(jnp.concatenate([*m_late, jnp.zeros_like(turned[0])], axis=0).T)
    sides = tuple(jnp.concatenate(both_sides, axis=1) for both_sides in zip(coeff, m_late))
    block, columns = 256, z_full.shape[1]

    def take_off(first, last):
        for index in range(first, last):
            at = pl.ds(index * block, block)
            v = tuple(ref[:, :, at].reshape(PLANES * SLAB, block) for ref in (v_hi, v_lo))
            share = product(v, sides, TN)
            z_full[at] = z_full[at] - share[:, :columns]
            u_hi[at], u_lo[at] = split(share[:, columns:])

    give_back(2)
    gather(4)
    take_off(0, 4)
    give_back(3)
    take_off(4, 8)
    z_late[3 * SLAB :] = jnp.zeros_like(z_late[3 * SLAB :])
    collect_late(2, 0)
    collect_late(3, SLAB)
    w_hi[: 2 * SLAB], w_lo[: 2 * SLAB] = split(z_late[: 2 * SLAB])

    for step in range(4):
        for way in range(2):
            for half in range(2):
                if step < 3 or half == way:
                    ring(way, step, half).wait_send()
    from_mates(t_all, 0).wait_send()
    from_mates(g_take, 1).wait_send()
    from_mates(g_all, 2).wait_send()
    from_planes(t_planes, 0).wait_send()
    from_planes(g_planes, 1).wait_send()
    for part in range(count):
        from_others(part, 1).wait_send()
        from_others(part, 2).wait_send()
        if part < LAST:
            mix_copy(part).wait_send()
            back_copy(part).wait_send()
    collect_late(4, 2 * SLAB)
    w_hi[2 * SLAB :], w_lo[2 * SLAB :] = split(z_late[2 * SLAB :])


def finish(part, u_hi, u_lo, w_hi, w_lo, out, stage, sem):
    block = stage.shape[1]
    w = jnp.concatenate([w_hi[...], w_hi[...], w_lo[...]], axis=0)
    copies = []
    for index in range(stage.shape[0]):
        at = pl.ds(index * block, block)
        u = jnp.concatenate([u_hi[at], u_lo[at], u_hi[at]], axis=1)
        stage[index] = part[at] - lax.dot_general(u, w, NN, preferred_element_type=F32)
        copies.append(pltpu.make_async_copy(stage.at[index], out.at[at], sem.at[index]))
        copies[-1].start()
    for copy in copies:
        copy.wait()


def shards(eigvecs, reflectors, factors):
    rows, columns = eigvecs.shape
    width = PLANES * SLAB // 2
    scratch = [
        pltpu.VMEM((PLANES, SLAB, rows), F32),
        pltpu.VMEM((PLANES, SLAB, rows), BF16),
        pltpu.VMEM((PLANES, SLAB, rows), BF16),
        pltpu.VMEM((rows, columns), BF16),
        pltpu.VMEM((rows, columns), BF16),
        pltpu.VMEM((PLANES, SLAB, columns), F32),
        pltpu.VMEM((4 * SLAB, columns), F32),
        pltpu.VMEM((SLAB, width), F32),
        pltpu.VMEM((ROWS, 4, 128), F32),
        pltpu.VMEM((PLANES, 4, 128), F32),
        pltpu.VMEM((ROWS, PLANES, 4, 128), F32),
        pltpu.VMEM((PLANES * SLAB, width), F32),
        pltpu.VMEM((ROWS, 4, 128), F32),
        pltpu.VMEM((ROWS, 4, 128), F32),
        pltpu.VMEM((PLANES, 4, 128), F32),
        pltpu.VMEM((ROWS, PLANES, 4, 128), F32),
        pltpu.VMEM((PLANES, 2 * SLAB, 2 * SLAB), F32),
        pltpu.VMEM((PLANES * SLAB, width), F32),
        pltpu.VMEM((PLANES, SLAB, PLANES * SLAB), F32),
        pltpu.SemaphoreType.DMA((3,)),
        pltpu.SemaphoreType.DMA((2, 4, 2)),
        pltpu.SemaphoreType.DMA((2, 4, 2)),
        pltpu.SemaphoreType.DMA((2, 2)),
        pltpu.SemaphoreType.DMA((2, 3)),
        pltpu.SemaphoreType.DMA((len(PARTS), 4)),
        pltpu.SemaphoreType.DMA((len(PARTS), 4)),
    ]
    early, last = HEIGHTS[:-1], pltpu.VMEM((ROWS, HEIGHTS[-1], 128), F32)
    paired = [pltpu.VMEM((2, CHIPS, height, 128), F32) for height in early]
    single = [pltpu.VMEM((CHIPS, height, 128), F32) for height in early]
    scratch += [*paired, last, *single, last, *paired, last, *paired]
    held = pl.pallas_call(
        kernel,
        out_shape=[
            jax.ShapeDtypeStruct((rows, columns), F32),
            jax.ShapeDtypeStruct((rows, 4 * SLAB), BF16),
            jax.ShapeDtypeStruct((rows, 4 * SLAB), BF16),
            jax.ShapeDtypeStruct((4 * SLAB, columns), BF16),
            jax.ShapeDtypeStruct((4 * SLAB, columns), BF16),
        ],
        in_specs=[pl.BlockSpec(memory_space=pltpu.HBM)] * 3,
        out_specs=[pl.BlockSpec(memory_space=pltpu.VMEM)] * 5,
        scratch_shapes=scratch,
        compiler_params=pltpu.CompilerParams(
            collective_id=0, has_side_effects=True, vmem_limit_bytes=40 * 1024 * 1024
        ),
    )(*(pltpu.with_memory_space_constraint(array, pltpu.HBM) for array in (eigvecs, reflectors.T, factors)))
    blocks = 8
    return pl.pallas_call(
        finish,
        out_shape=jax.ShapeDtypeStruct((rows, columns), F32),
        in_specs=[pl.BlockSpec(memory_space=pltpu.VMEM)] * 5,
        out_specs=pl.BlockSpec(memory_space=pltpu.HBM),
        scratch_shapes=[
            pltpu.VMEM((blocks, rows // blocks, columns), F32),
            pltpu.SemaphoreType.DMA((blocks,)),
        ],
        compiler_params=pltpu.CompilerParams(vmem_limit_bytes=32 * 1024 * 1024),
    )(*held)


def solution(mesh):
    return jax.shard_map(
        shards,
        mesh=mesh,
        in_specs=(P("prow", "pcol"), P("prow", "pcol"), P("pcol", None)),
        out_specs=P("prow", "pcol"),
        check_vma=False,
    )
```
